32 devices in a mesh: groups: 2 (over y), replica: 16 (over z, x, core), tensor: 1.
Axes of the slice: x: 2, y: 2, z: 4, core: 2. Of those that a mesh axis runs over, the one named last changes fastest.
Arguments:
- tokens: bfloat16 [8192, 8192], P(('groups', 'replica'), 'tensor'), parts along dimension 0, may hold values from -6 to 6
- row_adapter_index: int32 [8192], P(('groups', 'replica')), parts along dimension 0, may hold values from 0 to 255, as said below
- base_value_weight: bfloat16 [8192, 1024], P('tensor'), may hold values from -0.0625 to 0.0625
- down_factors: bfloat16 [256, 64, 8192], P('replica', None, 'tensor'), may hold values from -0.0625 to 0.0625
- up_factors: bfloat16 [256, 64, 1024], P('replica', None, 'tensor'), may hold values from -0.75 to 0.75
- adapter_scales: float32 [256], P('replica'), may hold values from 0.25 to 2
Outputs:
- values: bfloat16 [8192, 1024], P(('groups', 'replica'), 'tensor'), parts along dimension 0
The draws below stay inside these ranges and needn't reach their ends.
There are 2 independent parts, one for each index of `groups`. The reference program is written for one: setup_inputs(seed, part) draws one part's arguments, and reference() takes and returns one part's arrays. A program takes and returns all parts, laid end to end along the dimension named above; an argument that names none is the same for every part. Nothing has to cross between parts.
Inputs may be any that keep to these rules, and one draw needn't show every extreme that they name: `row_adapter_index`: adapter a is held by replica a // 16. Of the 256 rows of one replica, at most 48 name adapters held by any one replica, and in every draw every replica has some holder that its rows name exactly 48 times.
All inputs are finite; a program needn't handle non-finite values.
Results may differ from the reference program's by a relative error of at most 0.0042.
Values may be sent and summed in bfloat16 or wider, within the bound.
No kernel may reach another device: no remote copies, remote signals or barrier semaphores. Data moves between devices by JAX's collectives and lax.ppermute only.
A program may use at most 128 MiB of HBM per device.

```python
import math
import jax
import jax.numpy as jnp
from jax import lax

MODEL_WIDTH = 8192
VALUE_WIDTH = 1024
ADAPTER_RANK = 64
ADP_REP = 16
ROWS_REP = 256
ADAPTER_COUNT = 256
ROWS = 4096
CAP = 48
N_REPLICA = 16


def draw_row_adapter_index(key, part):
    key = jax.random.fold_in(key, 7)
    k_weight, k_noise, k_forced, k_local, k_order = jax.random.split(key, 5)
    slots = N_REPLICA * CAP
    slot_dest = jnp.arange(slots, dtype=jnp.int32) // CAP
    weight = jax.random.randint(k_weight, (N_REPLICA, N_REPLICA), 0, 4)
    noise = jax.random.randint(k_noise, (N_REPLICA, slots), 0, 1 << 16)
    score = noise + weight[:, slot_dest] * (1 << 15)
    forced = jax.random.randint(k_forced, (N_REPLICA,), 0, N_REPLICA)
    score = jnp.where(slot_dest[None, :] == forced[:, None], 0, score)
    score = score * slots + jnp.arange(slots, dtype=jnp.int32)[None, :]
    taken = jnp.argsort(score, axis=1)[:, :ROWS_REP]
    holder = taken // CAP
    local_block = jax.random.randint(k_local, (N_REPLICA, ROWS_REP), 0, ADP_REP)
    adapter_indices = holder * ADP_REP + local_block
    shuffle = jax.random.randint(k_order, (N_REPLICA, ROWS_REP), 0, 1 << 20)
    shuffle = shuffle * ROWS_REP + jnp.arange(ROWS_REP, dtype=jnp.int32)[None, :]
    order = jnp.argsort(shuffle, axis=1)
    adapter_indices = jnp.take_along_axis(adapter_indices, order, axis=1)
    return adapter_indices.reshape(ROWS).astype(jnp.int32)


def shard_levels(own_key, extent, pieces, least, top_value):
    loudness = 1.0
    for position, shards_of in pieces:
        draws = jax.random.uniform(jax.random.fold_in(jax.random.fold_in(own_key, 6), position), (shards_of,), jnp.float32, least / len(pieces), top_value / len(pieces))
        loudness = loudness * jnp.repeat(jnp.exp(draws), extent[position] // shards_of).reshape((-1,) + (1,) * (len(extent) - 1 - position))
    return loudness


def normal_values(own_key, shape, width, most, pieces=(), kind=jnp.bfloat16):
    array = jax.random.normal(own_key, shape, jnp.float32) * width
    if len(pieces) > 0:
        array = shard_levels(own_key, shape, pieces, -0.22, 0.18) * array
    return jnp.clip(array, min=-most, max=most).astype(kind)


def setup_inputs(seed: int = 0, part: int = 0) -> dict:
    arg_keys = jax.random.split(jax.random.key(seed), 7)
    part_splits = jax.random.split(jax.random.fold_in(arg_keys[6], part), 7)
    return {
        "tokens": normal_values(part_splits[0], (ROWS, MODEL_WIDTH), 1.0, 6.0, ((0, 16),)),
        "row_adapter_index": draw_row_adapter_index(jax.random.fold_in(jax.random.fold_in(arg_keys[6], part), 71), part),
        "base_value_weight": normal_values(arg_keys[2], (MODEL_WIDTH, VALUE_WIDTH), MODEL_WIDTH ** -0.5, 0.0625),
        "down_factors": normal_values(arg_keys[3], (ADAPTER_COUNT, ADAPTER_RANK, MODEL_WIDTH), MODEL_WIDTH ** -0.5, 0.0625, ((0, 16),)),
        "up_factors": normal_values(arg_keys[4], (ADAPTER_COUNT, ADAPTER_RANK, VALUE_WIDTH), ADAPTER_RANK ** -0.5, 0.75, ((0, 16),)),
        "adapter_scales": jnp.clip(jnp.exp(math.log(2.0) - 2.0794415 * jax.random.uniform(arg_keys[5], (ADAPTER_COUNT,), jnp.float32) ** shard_levels(arg_keys[5], (ADAPTER_COUNT,), ((0, 16),), -0.2, 0.2)), 0.25, 2.0),
    }


def reference(tokens, row_adapter_index, base_value_weight, down_factors, up_factors, adapter_scales):
    base = jnp.dot(tokens, base_value_weight, preferred_element_type=jnp.float32)
    blocks = ROWS // 32
    token_blocks = tokens.reshape(blocks, 32, MODEL_WIDTH)
    id_blocks = row_adapter_index.reshape(blocks, 32)

    def one_block(pair):
        input_rows, adapter_indices = pair
        down_factor_rows = down_factors[adapter_indices].astype(jnp.float32)
        low_rank_output = jnp.einsum("vi,vti->vt", input_rows.astype(jnp.float32), down_factor_rows)
        scaled_output = (low_rank_output * adapter_scales[adapter_indices][:, None]).astype(jnp.bfloat16)
        up_factor_rows = up_factors[adapter_indices].astype(jnp.float32)
        return jnp.einsum("bk,bkh->bh", scaled_output.astype(jnp.float32), up_factor_rows)

    delta = lax.map(one_block, (token_blocks, id_blocks)).reshape(ROWS, VALUE_WIDTH)
    return (base + delta).astype(jnp.bfloat16)
```

```python
import jax
import jax.numpy as jnp
from jax import lax
from jax.sharding import PartitionSpec as P


def tiers_for(rows, cap):
    chip_rows = 2 * rows
    unit = chip_rows // 32
    listed = [(19, 15, 10, 6), (21, 17, 12, 6), (24, 19, 13, 8)]
    return [tuple(unit * s for s in t) for t in listed] + [
        (chip_rows, chip_rows, min(chip_rows, 2 * cap), cap)
    ]


def by_ring(tokens, row_adapter_index, base_value_weight, down_factors, up_factors, adapter_scales):
    rows, width = tokens.shape
    own_adapters, rank, _ = down_factors.shape
    cols = base_value_weight.shape[1]
    half, half_cols = width // 2, cols // 2
    peers = lax.axis_size("replica")
    chips = peers // 2
    lines = chips // 2
    hops = chips // 2
    adapters = 2 * own_adapters
    chip_rows = 2 * rows
    cap = 4 * (3 * rows // peers)
    me = lax.axis_index("replica")
    core = me % 2
    chip = me // 2
    order = [2 * z for z in range(lines)] + [2 * z + 1 for z in reversed(range(lines))]

    def place(c):
        return jnp.where(c % 2 == 0, c // 2, chips - 1 - c // 2)

    def across(v):
        return lax.ppermute(v, "replica", [(i, i ^ 1) for i in range(peers)])

    def around(v, step):
        moves = [
            (2 * order[p] + c, 2 * order[(p + step) % chips] + c)
            for p in range(chips)
            for c in range(2)
        ]
        return lax.ppermute(v, "replica", moves)

    def first_core_first(mine, other, axis=0):
        return jnp.where(
            core == 0,
            jnp.concatenate([mine, other], axis),
            jnp.concatenate([other, mine], axis),
        )

    def own_first(v):
        return jnp.where(core == 0, v, jnp.roll(v, v.shape[0] // 2, 0))

    with jax.named_scope("counts"):
        distance_own = (place(row_adapter_index // adapters) - place(chip)) % chips
        own_counts = jnp.sum(
            (distance_own[:, None] == jnp.arange(chips)[None, :]).astype(jnp.int32), axis=0
        )
        all_counts = lax.all_gather(own_counts, ("groups", "replica"), axis=0)
        counts = jnp.sum(all_counts.reshape(-1, 2, chips), axis=1)
    with jax.named_scope("cores"):
        index = first_core_first(row_adapter_index, across(row_adapter_index))
        mine_at, other_at = core * half, (1 - core) * half
        features = jnp.concatenate(
            [
                lax.dynamic_slice_in_dim(tokens, mine_at, half, 1),
                across(lax.dynamic_slice_in_dim(tokens, other_at, half, 1)),
            ],
            0,
        )
        down = jnp.concatenate(
            [
                lax.dynamic_slice_in_dim(down_factors, mine_at, half, 2),
                across(lax.dynamic_slice_in_dim(down_factors, other_at, half, 2)),
            ],
            0,
        ).reshape(adapters * rank, half)
        up = jnp.concatenate(
            [
                lax.dynamic_slice_in_dim(up_factors, core * half_cols, half_cols, 2),
                across(lax.dynamic_slice_in_dim(up_factors, (1 - core) * half_cols, half_cols, 2)),
            ],
            0,
        ).reshape(adapters * rank, half_cols)
        scales = jnp.concatenate([adapter_scales, across(adapter_scales)], 0)
    with jax.named_scope("ranks"):
        distance = (place(index // adapters) - place(chip)) % chips
        local = index % adapters
        marks = (distance[:, None] == jnp.arange(chips)[None, :]).astype(jnp.bfloat16)
        earlier = jnp.tril(jnp.ones((chip_rows, chip_rows), jnp.bfloat16), -1)
        ahead = jnp.dot(earlier, marks, preferred_element_type=jnp.float32)
        rank_in = jnp.sum(ahead * marks.astype(jnp.float32), axis=1).astype(jnp.int32)
        mine_counts = jnp.sum(marks.astype(jnp.int32), axis=0)

    tiers = tiers_for(rows, cap)

    def sums(c, direction):
        at = lambda h: c[..., h] if direction > 0 else c[..., chips - h]
        total, out = jnp.zeros_like(c[..., 0]), []
        for h in range(hops - 1, 0, -1):
            total = total + at(h)
            out.append(total)
        return out[::-1]

    def slack(c, tier, direction):
        room = jnp.full_like(c[..., 0], tier[-1])
        for h, n in enumerate(sums(c, direction)):
            room = jnp.minimum(room, tier[h] - n)
        return room

    with jax.named_scope("tier"):
        fits = []
        for tier in tiers[:-1]:
            right, left = slack(counts, tier, 1), slack(counts, tier, -1)
            fits.append(
                jnp.all((right >= 0) & (left >= 0) & (right + left >= counts[:, hops]))
            )
        fits.append(jnp.bool_(True))
        choice = jnp.argmax(jnp.stack(fits).astype(jnp.int32))

    def exchange(tier, features, down, up, scales, distance, local, rank_in, c):
        windows = [min(cap, s) for s in tier]
        right_room, left_room = slack(c, tier, 1), slack(c, tier, -1)
        right_sums, left_sums = sums(c, 1), sums(c, -1)
        balance = (sum(left_sums) - sum(right_sums) + hops * c[hops]) // (2 * hops)
        split = jnp.clip(balance, jnp.maximum(c[hops] - left_room, 0), jnp.minimum(right_room, c[hops]))
        tail = c[hops] - split
        right_at_least = [n + split for n in right_sums] + [split]
        left_at_least = [n + tail for n in left_sums] + [tail]
        far = distance == hops
        goes_right = ((distance > 0) & (distance < hops)) | (far & (rank_in < split))
        goes_left = (distance > hops) | (far & (rank_in >= split))
        right_need = distance
        left_need = chips - distance
        zero = jnp.zeros_like(c[0])

        def positions(goes, need, at_least, rank):
            start = jnp.zeros_like(rank)
            bounds = at_least + [zero]
            for h in range(1, hops):
                start = jnp.where(need == h, bounds[h], start)
            return jnp.where(goes, start + rank, -1)

        right_pos = positions(goes_right, right_need, right_at_least, rank_in)
        left_pos = positions(
            goes_left, left_need, left_at_least, jnp.where(far, rank_in - split, rank_in)
        )
        own_pos = jnp.where(distance == 0, rank_in, -1)

        def packed(pos, size):
            hit = jnp.arange(size, dtype=jnp.int32)[:, None] == own_first(pos)[None, :]
            return jnp.dot(
                hit.astype(jnp.bfloat16), features, preferred_element_type=jnp.float32
            ).astype(jnp.bfloat16)

        def labelled(pos, size, need):
            hit = jnp.arange(size, dtype=jnp.int32)[:, None] == pos[None, :]
            return jnp.sum(jnp.where(hit, (need * adapters + local + 1)[None, :], 0), axis=1) - 1

        def low_of(x, label, need):
            mine = (label >= need * adapters) & (label < (need + 1) * adapters)
            slot = label - need * adapters
            slot = jnp.where(core == 0, slot, (slot + own_adapters) % adapters)
            chosen = mine[:, None] & (slot[:, None] == jnp.arange(adapters)[None, :])
            wide = lax.dot_general(
                x, down, (((1,), (1,)), ((), ())), preferred_element_type=jnp.float32
            )
            low = jnp.sum(
                wide.reshape(x.shape[0], adapters, rank) * chosen.astype(jnp.float32)[:, :, None],
                axis=1,
            )
            return low, chosen

        def finish(low, chosen):
            total = low + across(low)
            factor = jnp.sum(jnp.where(chosen, scales[None, :], 0.0), axis=1)
            scaled = (total * factor[:, None]).astype(jnp.bfloat16)
            spread = (scaled[:, None, :] * chosen.astype(jnp.bfloat16)[:, :, None]).reshape(
                -1, adapters * rank
            )
            return jnp.dot(spread, up, preferred_element_type=jnp.float32).astype(jnp.bfloat16)

        right, right_label = packed(right_pos, tier[0]), labelled(right_pos, tier[0], right_need)
        left, left_label = packed(left_pos, tier[0]), labelled(left_pos, tier[0], left_need)
        own = packed(own_pos, cap)
        own_label = labelled(own_pos, cap, jnp.zeros_like(distance))
        deltas = [finish(*low_of(own, own_label, 0))]
        places = jnp.where(distance == 0, rank_in, -1)
        base_slot = cap
        for h in range(1, hops + 1):
            size, window = tier[h - 1], windows[h - 1]
            right = around(right[:size], 1)
            right_label = around(right_label[:size], 1)
            left = around(left[:size], -1)
            left_label = around(left_label[:size], -1)
            results = []
            for block, label in ((right, right_label), (left, left_label)):
                beyond = jnp.sum((label >= (h + 1) * adapters).astype(jnp.int32))
                at = jnp.minimum(beyond, size - window)
                x = lax.dynamic_slice_in_dim(block, at, window, 0)
                lab = lax.dynamic_slice_in_dim(label, at, window, 0)
                results.append(low_of(x, lab, h))
            low = jnp.concatenate([results[0][0], results[1][0]], 0)
            chosen = jnp.concatenate([results[0][1], results[1][1]], 0)
            delta = finish(low, chosen)
            deltas.append(around(delta[:window], -h))
            deltas.append(around(delta[window:], h))
            for pos, need, goes, at_least in (
                (right_pos, right_need, goes_right, right_at_least),
                (left_pos, left_need, goes_left, left_at_least),
            ):
                beyond = at_least[h] if h < hops else zero
                at = jnp.minimum(beyond, size - window)
                places = jnp.where(goes & (need == h), base_slot + pos - at, places)
                base_slot += window
        hit = places[:, None] == jnp.arange(base_slot, dtype=jnp.int32)[None, :]
        return jnp.dot(
            hit.astype(jnp.bfloat16),
            jnp.concatenate(deltas, 0),
            preferred_element_type=jnp.float32,
        ).astype(jnp.bfloat16)

    base = jnp.dot(tokens, base_value_weight, preferred_element_type=jnp.float32)
    branches = [lambda *a, tier=tier: exchange(tier, *a) for tier in tiers]
    delta = lax.switch(
        choice, branches, features, down, up, scales, distance, local, rank_in, mine_counts
    )
    kept = lax.dynamic_slice_in_dim(delta, core * rows, rows, 0)
    given = across(lax.dynamic_slice_in_dim(delta, (1 - core) * rows, rows, 0))
    return (base + first_core_first(kept, given, 1).astype(jnp.float32)).astype(jnp.bfloat16)


def by_all_to_all(
    tokens, row_adapter_index, base_value_weight, down_factors, up_factors, adapter_scales
):
    peers = lax.axis_size("replica")
    input_rows = tokens.shape[0]
    feature_width = tokens.shape[1]
    rows_per_replica = down_factors.shape[0]
    rank_index = down_factors.shape[1]
    capacity = 3 * input_rows // peers
    slots = peers * capacity
    holder = row_adapter_index // rows_per_replica
    local_slot = row_adapter_index % rows_per_replica
    dest_table = (holder[:, None] == jnp.arange(peers, dtype=jnp.int32)[None, :]).astype(jnp.int32)
    position = jnp.sum(jnp.cumsum(dest_table, axis=0) * dest_table, axis=1) - 1
    target = holder * capacity + position
    outbox = jnp.zeros((slots, feature_width), tokens.dtype).at[target].set(tokens)
    labels = jnp.full((slots,), -1, jnp.int32).at[target].set(local_slot)
    inbox, in_labels = (
        lax.all_to_all(
            outbox.reshape(peers, capacity, feature_width),
            "replica",
            split_axis=0,
            concat_axis=0,
            tiled=True,
        ),
        lax.all_to_all(
            labels.reshape(peers, capacity), "replica", split_axis=0, concat_axis=0, tiled=True
        ),
    )
    received = inbox.reshape(slots, feature_width)
    marks = in_labels.reshape(slots)
    selected_adapters = (
        marks[:, None] == jnp.arange(rows_per_replica, dtype=jnp.int32)[None, :]
    ).astype(jnp.float32)
    stacked_down_factors = down_factors.reshape(rows_per_replica * rank_index, feature_width)
    wide = lax.dot_general(
        received, stacked_down_factors, (((1,), (1,)), ((), ())), preferred_element_type=jnp.float32
    )
    partial_low = jnp.sum(
        wide.reshape(slots, rows_per_replica, rank_index) * selected_adapters[:, :, None], axis=1
    )
    low_rank_output = lax.psum(partial_low, "tensor")
    scale_factor = jnp.sum(selected_adapters * adapter_scales[None, :], axis=1)
    scaled_output = (low_rank_output * scale_factor[:, None]).astype(jnp.bfloat16)
    spread_rows = (
        scaled_output[:, None, :] * selected_adapters[:, :, None].astype(jnp.bfloat16)
    ).reshape(slots, rows_per_replica * rank_index)
    delta = jnp.dot(
        spread_rows,
        up_factors.reshape(rows_per_replica * rank_index, up_factors.shape[2]),
        preferred_element_type=jnp.float32,
    )
    base_part = jnp.dot(received, base_value_weight, preferred_element_type=jnp.float32)
    base_cols = lax.psum_scatter(base_part, "tensor", scatter_dimension=1, tiled=True)
    finished = base_cols + delta
    returned = lax.all_to_all(
        finished.reshape(peers, capacity, finished.shape[1]).astype(jnp.bfloat16),
        "replica",
        split_axis=0,
        concat_axis=0,
        tiled=True,
    ).astype(jnp.float32)
    total = returned.reshape(slots, finished.shape[1])[target]
    return total.astype(jnp.bfloat16)


def solution(mesh):
    in_specs = (
        P(("groups", "replica"), "tensor"),
        P(("groups", "replica")),
        P("tensor", None),
        P("replica", None, "tensor"),
        P("replica", None, "tensor"),
        P("replica"),
    )
    out_specs = P(("groups", "replica"), "tensor")
    whole_rows = mesh.shape["tensor"] == 1 and mesh.shape["replica"] % 4 == 0
    return jax.shard_map(
        by_ring if whole_rows else by_all_to_all,
        mesh=mesh,
        in_specs=in_specs,
        out_specs=out_specs,
        check_vma=False,
    )
```

```python
import jax
import jax.numpy as jnp
from jax import lax
from jax.sharding import PartitionSpec as P


def tiers_for(rows, cap):
    chip_rows = 2 * rows
    unit = chip_rows // 32
    listed = [(19, 15, 10, 6), (21, 17, 11, 6), (24, 19, 13, 8)]
    return [tuple(unit * s for s in t) for t in listed] + [
        (chip_rows, chip_rows, min(chip_rows, 2 * cap), cap)
    ]


def by_ring(tokens, row_adapter_index, base_value_weight, down_factors, up_factors, adapter_scales):
    rows, width = tokens.shape
    own_adapters, rank, _ = down_factors.shape
    cols = base_value_weight.shape[1]
    half, half_cols = width // 2, cols // 2
    peers = lax.axis_size("replica")
    chips = peers // 2
    lines = chips // 2
    hops = chips // 2
    adapters = 2 * own_adapters
    chip_rows = 2 * rows
    cap = 4 * (3 * rows // peers)
    tiers = tiers_for(rows, cap)
    me = lax.axis_index("replica")
    core = me % 2
    order = [2 * z for z in range(lines)] + [2 * z + 1 for z in reversed(range(lines))]

    def place(c):
        return jnp.where(c % 2 == 0, c // 2, chips - 1 - c // 2)

    here = place(me // 2)

    def across(v):
        return lax.ppermute(v, "replica", [(i, i ^ 1) for i in range(peers)])

    def around(v, step):
        moves = [
            (2 * order[p] + c, 2 * order[(p + step) % chips] + c)
            for p in range(chips)
            for c in range(2)
        ]
        return lax.ppermute(v, "replica", moves)

    with jax.named_scope("halves"):
        mine = lax.dynamic_slice_in_dim(tokens, core * half, half, 1)
        other = across(lax.dynamic_slice_in_dim(tokens, (1 - core) * half, half, 1))
        features = jnp.concatenate([mine, other], 0)

    with jax.named_scope("slots"):
        index = jnp.concatenate([row_adapter_index, across(row_adapter_index)], 0)
        distance = (place(index // adapters) - here) % chips
        local = index % adapters
        spot = jnp.arange(chip_rows, dtype=jnp.int32)
        canonical = jnp.where(core == 0, spot, (spot + rows) % chip_rows)
        marks = distance[:, None] == jnp.arange(chips)[None, :]
        earlier = (canonical[None, :] < canonical[:, None]).astype(jnp.bfloat16)
        ahead = jnp.dot(earlier, marks.astype(jnp.bfloat16), preferred_element_type=jnp.float32)
        marks_f = marks.astype(jnp.float32)
        rank_in = jnp.sum(ahead * marks_f, axis=1, keepdims=True)
        count = jnp.sum(marks_f, axis=0, keepdims=True)
        weigh = jnp.asarray(
            [[0.0] + [-float(k) for k in range(1, hops)] + [float(hops)]
             + [float(chips - k) for k in range(hops + 1, chips)]], jnp.float32)
        level = jnp.arange(1, hops)[:, None]
        kind = jnp.arange(chips)[None, :]
        right_sums = jnp.sum(count * ((kind >= level) & (kind < hops)), axis=1, keepdims=True)
        left_sums = jnp.sum(count * ((chips - kind >= level) & (kind > hops)), axis=1, keepdims=True)
        nominal = jnp.asarray(tiers[1][:-1], jnp.float32)[:, None]
        farthest = float(tiers[1][-1])
        at_far = count[:, hops : hops + 1]
        right_room = jnp.minimum(jnp.min(nominal - right_sums, axis=0, keepdims=True), farthest)
        left_room = jnp.minimum(jnp.min(nominal - left_sums, axis=0, keepdims=True), farthest)
        split = jnp.floor(jnp.sum(weigh * count, axis=1, keepdims=True) / (2.0 * hops))
        split = jnp.minimum(jnp.maximum(split, at_far - left_room), right_room)
        split = jnp.clip(split, 0.0, at_far)
        right_n = jnp.concatenate([right_sums + split, split], 0)
        left_n = jnp.concatenate([left_sums + at_far - split, at_far - split], 0)
        column = jnp.arange(chips)[:, None]
        before = ((kind < hops) & (column > kind) & (column < hops) & (kind > 0)) | (
            (kind > hops) & (column > hops) & (column < kind)
        )
        start = jnp.sum(count.reshape(chips, 1) * before, axis=0, keepdims=True)
        start = start + jnp.where((kind > 0) & (kind < hops), split, 0.0)
        start = start + jnp.where(kind > hops, at_far - split, 0.0)
        side = jnp.where(kind == 0, 2.0 * chip_rows, jnp.where(kind > hops, 1.0 * chip_rows, 0.0))
        slot = jnp.sum(marks_f * (start + side), axis=1, keepdims=True) + rank_in
        turned = marks[:, hops : hops + 1] & (rank_in >= split)
        slot = (slot + jnp.where(turned, chip_rows - split, 0.0)).astype(jnp.int32)[:, 0]

    with jax.named_scope("metadata"):
        item = jnp.arange(cap, dtype=jnp.int32)
        listed = jnp.sum(
            jnp.where(
                (rank_in[:, 0].astype(jnp.int32)[None, None, :] == item[None, :, None])
                & marks.T[:, None, :],
                local[None, None, :] + 1,
                0,
            ),
            axis=2,
        )
        far_kind = kind == hops
        right_start = jnp.where(far_kind, 0.0, start)
        right_end = jnp.where(far_kind, split, start + count)
        left_start = jnp.where(far_kind, -split, start)
        left_end = jnp.where(far_kind, at_far - split, start + count)
        most = jnp.maximum(right_n, left_n)
        head = jnp.concatenate(
            [right_start, right_end, left_start, left_end]
            + [jnp.broadcast_to(most[h : h + 1], (1, chips)) for h in range(hops)],
            0,
        ).astype(jnp.int32).T
        table = jnp.concatenate([head, listed], 1)
        lanes = table.shape[1]
        target = (place(jnp.arange(peers, dtype=jnp.int32) // 2) - here) % chips
        outgoing = jnp.sum(
            jnp.where((target[:, None] == jnp.arange(chips)[None, :])[:, :, None], table[None], 0),
            axis=1,
        )
        groups = lax.axis_size("groups")
        outgoing = jnp.broadcast_to(outgoing[None], (groups, peers, lanes)).reshape(-1, lanes)
        incoming = lax.all_to_all(
            outgoing, ("groups", "replica"), split_axis=0, concat_axis=0, tiled=True
        )
        needed = jnp.max(incoming[:, 4 : 4 + hops], axis=0, keepdims=True)
        holds = jnp.all(needed <= jnp.asarray(tiers[:-1], jnp.int32), axis=1)
        choice = jnp.minimum(jnp.sum((jnp.cumsum(holds.astype(jnp.int32)) == 0).astype(jnp.int32)), len(tiers) - 1)
        incoming = lax.dynamic_slice_in_dim(incoming, lax.axis_index("groups") * peers, peers, 0)
        source = place(jnp.arange(peers, dtype=jnp.int32) // 2)
        same_core = (jnp.arange(peers) % 2) == core
        back = (here - source) % chips
        chosen_source = (back[None, :] == jnp.arange(chips)[:, None]) & same_core[None, :]
        heard = jnp.sum(jnp.where(chosen_source[:, :, None], incoming[None], 0), axis=1)

    def exchange(tier, features, slot, heard, tokens, weight, down_factors, up_factors, own_scales):
        low_bound = list(tier[1:]) + [0]

        def packed(base, first, size):
            hit = (base + first + jnp.arange(size, dtype=jnp.int32))[:, None] == slot[None, :]
            return jnp.dot(
                hit.astype(jnp.bfloat16), features, preferred_element_type=jnp.float32
            ).astype(jnp.bfloat16)

        def segment(direction, h):
            first = low_bound[h - 1]
            size = tier[h - 1] - first
            if size == 0:
                return None
            return packed(0 if direction > 0 else chip_rows, first, size)

        ways = (1, -1)
        start_segments = {(d, s): segment(d, s) for s in range(hops, 1, -1) for d in ways}
        started = [v for v in start_segments.values() if v is not None]
        tokens, weight, down_factors, up_factors, own_scales, *_ = lax.optimization_barrier(
            (tokens, weight, down_factors, up_factors, own_scales, *started)
        )
        arrived = {}
        for h in range(1, hops + 1):
            for s in range(hops, max(h, 2) - 1, -1):
                for d in ways:
                    v = start_segments[d, s] if h == 1 else arrived[h - 1, d, s]
                    arrived[h, d, s] = None if v is None else around(v, d)
        late = [v for k, v in arrived.items() if k[0] == hops - 1 and v is not None]
        late_slot, *_ = lax.optimization_barrier((slot, *late))
        slot_now, slot = slot, late_slot
        for d in ways:
            v = segment(d, 1)
            arrived[1, d, 1] = None if v is None else around(v, d)
        slot = slot_now

        with jax.named_scope("weights"):
            down = jnp.concatenate(
                [
                    lax.dynamic_slice_in_dim(down_factors, core * half, half, 2),
                    across(lax.dynamic_slice_in_dim(down_factors, (1 - core) * half, half, 2)),
                ],
                0,
            ).reshape(adapters * rank, half)
            up = jnp.concatenate(
                [
                    lax.dynamic_slice_in_dim(up_factors, core * half_cols, half_cols, 2),
                    across(
                        lax.dynamic_slice_in_dim(up_factors, (1 - core) * half_cols, half_cols, 2)
                    ),
                ],
                0,
            ).reshape(adapters * rank, half_cols)
            scales = jnp.concatenate([own_scales, across(own_scales)], 0)
        base = jnp.dot(tokens, weight, preferred_element_type=jnp.float32)

        def labels(direction, h, first, size):
            row = heard[h if direction > 0 else chips - h]
            begin, end = (row[0], row[1]) if direction > 0 else (row[2], row[3])
            at = first + jnp.arange(size, dtype=jnp.int32)
            hit = (at - begin)[:, None] == item[None, :]
            label = jnp.sum(jnp.where(hit, row[4 + hops :][None, :], 0), axis=1) - 1
            return jnp.where(at < end, label, -1)

        def product(x, label):
            turned = jnp.where(core == 0, label, (label + own_adapters) % adapters)
            chosen = (label >= 0)[:, None] & (turned[:, None] == jnp.arange(adapters)[None, :])
            wide = lax.dot_general(
                x, down, (((1,), (1,)), ((), ())), preferred_element_type=jnp.float32
            )
            low = jnp.sum(
                wide.reshape(x.shape[0], adapters, rank) * chosen.astype(jnp.float32)[:, :, None],
                axis=1,
            )
            total = low + across(low)
            factor = jnp.sum(jnp.where(chosen, scales[None, :], 0.0), axis=1)
            scaled = (total * factor[:, None]).astype(jnp.bfloat16)
            spread = (scaled[:, None, :] * chosen.astype(jnp.bfloat16)[:, :, None]).reshape(
                -1, adapters * rank
            )
            return jnp.dot(spread, up, preferred_element_type=jnp.float32).astype(jnp.bfloat16)

        own_label = heard[0, 4 + hops :] - 1
        own_delta = product(packed(2 * chip_rows, 0, cap), own_label)

        def hop_product(h, segments):
            segments = [s for s in segments if arrived[h, 1, s] is not None]
            first = low_bound[segments[0] - 1]
            size = sum(arrived[h, 1, s].shape[0] for s in segments)
            x = jnp.concatenate([arrived[h, d, s] for d in ways for s in segments], 0)
            label = jnp.concatenate([labels(d, h, first, size) for d in ways], 0)
            delta = product(x, label)
            return delta[:size], delta[size:]

        back = None
        for h in range(hops, 0, -1):
            delta = list(hop_product(h, list(range(hops, max(h, 2) - 1, -1))))
            if back is not None:
                delta = [
                    v + jnp.pad(b, ((0, v.shape[0] - b.shape[0]), (0, 0)))
                    for v, b in zip(delta, back)
                ]
            back = [around(v, -d) for v, d in zip(delta, ways)]
        results = [[b] for b in back]
        if arrived[1, 1, 1] is not None:
            for k, v in enumerate(hop_product(1, [1])):
                results[k].append(around(v, -ways[k]))
        finished = jnp.concatenate(results[0] + results[1] + [own_delta], 0)
        column = jnp.where(
            slot < chip_rows,
            slot,
            jnp.where(slot < 2 * chip_rows, slot - chip_rows + tier[0], slot - 2 * chip_rows + 2 * tier[0]),
        )
        hit = (column[:, None] == jnp.arange(finished.shape[0], dtype=jnp.int32)[None, :]).astype(
            jnp.bfloat16
        )

        def taken(h):
            return jnp.dot(h, finished, preferred_element_type=jnp.float32).astype(jnp.bfloat16)

        given = across(taken(hit[rows:]))
        kept = taken(hit[:rows])
        delta = jnp.where(
            core == 0,
            jnp.concatenate([kept, given], 1),
            jnp.concatenate([given, kept], 1),
        )
        return (base + delta.astype(jnp.float32)).astype(jnp.bfloat16)

    branches = [lambda *a, tier=tier: exchange(tier, *a) for tier in tiers]
    return lax.switch(
        choice,
        branches,
        features,
        slot,
        heard,
        tokens,
        base_value_weight,
        down_factors,
        up_factors,
        adapter_scales,
    )


def by_all_to_all(
    tokens, row_adapter_index, base_value_weight, down_factors, up_factors, adapter_scales
):
    peers = lax.axis_size("replica")
    input_rows = tokens.shape[0]
    feature_width = tokens.shape[1]
    rows_per_replica = down_factors.shape[0]
    rank_index = down_factors.shape[1]
    capacity = 3 * input_rows // peers
    slots = peers * capacity
    holder = row_adapter_index // rows_per_replica
    local_slot = row_adapter_index % rows_per_replica
    dest_table = (holder[:, None] == jnp.arange(peers, dtype=jnp.int32)[None, :]).astype(jnp.int32)
    position = jnp.sum(jnp.cumsum(dest_table, axis=0) * dest_table, axis=1) - 1
    target = holder * capacity + position
    outbox = jnp.zeros((slots, feature_width), tokens.dtype).at[target].set(tokens)
    labels = jnp.full((slots,), -1, jnp.int32).at[target].set(local_slot)
    inbox, in_labels = (
        lax.all_to_all(
            outbox.reshape(peers, capacity, feature_width),
            "replica",
            split_axis=0,
            concat_axis=0,
            tiled=True,
        ),
        lax.all_to_all(
            labels.reshape(peers, capacity), "replica", split_axis=0, concat_axis=0, tiled=True
        ),
    )
    received = inbox.reshape(slots, feature_width)
    marks = in_labels.reshape(slots)
    selected_adapters = (
        marks[:, None] == jnp.arange(rows_per_replica, dtype=jnp.int32)[None, :]
    ).astype(jnp.float32)
    stacked_down_factors = down_factors.reshape(rows_per_replica * rank_index, feature_width)
    wide = lax.dot_general(
        received, stacked_down_factors, (((1,), (1,)), ((), ())), preferred_element_type=jnp.float32
    )
    partial_low = jnp.sum(
        wide.reshape(slots, rows_per_replica, rank_index) * selected_adapters[:, :, None], axis=1
    )
    low_rank_output = lax.psum(partial_low, "tensor")
    scale_factor = jnp.sum(selected_adapters * adapter_scales[None, :], axis=1)
    scaled_output = (low_rank_output * scale_factor[:, None]).astype(jnp.bfloat16)
    spread_rows = (
        scaled_output[:, None, :] * selected_adapters[:, :, None].astype(jnp.bfloat16)
    ).reshape(slots, rows_per_replica * rank_index)
    delta = jnp.dot(
        spread_rows,
        up_factors.reshape(rows_per_replica * rank_index, up_factors.shape[2]),
        preferred_element_type=jnp.float32,
    )
    base_part = jnp.dot(received, base_value_weight, preferred_element_type=jnp.float32)
    base_cols = lax.psum_scatter(base_part, "tensor", scatter_dimension=1, tiled=True)
    finished = base_cols + delta
    returned = lax.all_to_all(
        finished.reshape(peers, capacity, finished.shape[1]).astype(jnp.bfloat16),
        "replica",
        split_axis=0,
        concat_axis=0,
        tiled=True,
    ).astype(jnp.float32)
    total = returned.reshape(slots, finished.shape[1])[target]
    return total.astype(jnp.bfloat16)


def solution(mesh):
    in_specs = (
        P(("groups", "replica"), "tensor"),
        P(("groups", "replica")),
        P("tensor", None),
        P("replica", None, "tensor"),
        P("replica", None, "tensor"),
        P("replica"),
    )
    out_specs = P(("groups", "replica"), "tensor")
    whole_rows = mesh.shape["tensor"] == 1 and mesh.shape["replica"] % 4 == 0
    return jax.shard_map(
        by_ring if whole_rows else by_all_to_all,
        mesh=mesh,
        in_specs=in_specs,
        out_specs=out_specs,
        check_vma=False,
    )
```

```python
import jax
import jax.numpy as jnp
from jax import lax
from jax.sharding import PartitionSpec as P


def sizes_for(rows, cap):
    chip_rows = 2 * rows
    unit = chip_rows // 32
    usual = tuple(unit * s for s in (23, 17, 12, 6))
    return usual, (chip_rows, chip_rows, min(chip_rows, 2 * cap), cap)


def tied(*groups):
    flat = [v for g in groups for v in g]
    flat = list(lax.optimization_barrier(tuple(flat)))
    out = []
    for g in groups:
        out.append(flat[: len(g)])
        flat = flat[len(g) :]
    return out


def by_ring(tokens, row_adapter_index, base_value_weight, down_factors, up_factors, adapter_scales):
    rows, width = tokens.shape
    own_adapters, rank, _ = down_factors.shape
    cols = base_value_weight.shape[1]
    half, half_cols = width // 2, cols // 2
    peers = lax.axis_size("replica")
    chips = peers // 2
    lines = chips // 2
    hops = chips // 2
    adapters = 2 * own_adapters
    chip_rows = 2 * rows
    cap = 4 * (3 * rows // peers)
    usual, largest = sizes_for(rows, cap)
    me = lax.axis_index("replica")
    core = me % 2
    order = [2 * z for z in range(lines)] + [2 * z + 1 for z in reversed(range(lines))]

    def place(c):
        return jnp.where(c % 2 == 0, c // 2, chips - 1 - c // 2)

    here = place(me // 2)

    def across(v):
        return lax.ppermute(v, "replica", [(i, i ^ 1) for i in range(peers)])

    def around(v, step):
        moves = [
            (2 * order[p] + c, 2 * order[(p + step) % chips] + c)
            for p in range(chips)
            for c in range(2)
        ]
        return lax.ppermute(v, "replica", moves)

    with jax.named_scope("halves"):
        mine = lax.dynamic_slice_in_dim(tokens, core * half, half, 1)
        other = across(lax.dynamic_slice_in_dim(tokens, (1 - core) * half, half, 1))
        features = jnp.concatenate([mine, other], 0)

    with jax.named_scope("slots"):
        index = jnp.concatenate([row_adapter_index, across(row_adapter_index)], 0)
        distance = (place(index // adapters) - here) % chips
        local = index % adapters
        spot = jnp.arange(chip_rows, dtype=jnp.int32)
        canonical = jnp.where(core == 0, spot, (spot + rows) % chip_rows)
        marks = distance[:, None] == jnp.arange(chips)[None, :]
        earlier = (canonical[None, :] < canonical[:, None]).astype(jnp.bfloat16)
        ahead = jnp.dot(earlier, marks.astype(jnp.bfloat16), preferred_element_type=jnp.float32)
        marks_f = marks.astype(jnp.float32)
        rank_in = jnp.sum(ahead * marks_f, axis=1, keepdims=True)
        count = jnp.sum(marks_f, axis=0, keepdims=True)
        weigh = jnp.asarray(
            [[0.0] + [-float(k) for k in range(1, hops)] + [float(hops)]
             + [float(chips - k) for k in range(hops + 1, chips)]], jnp.float32)
        level = jnp.arange(1, hops)[:, None]
        kind = jnp.arange(chips)[None, :]
        right_sums = jnp.sum(count * ((kind >= level) & (kind < hops)), axis=1, keepdims=True)
        left_sums = jnp.sum(count * ((chips - kind >= level) & (kind > hops)), axis=1, keepdims=True)
        nominal = jnp.asarray(usual[:-1], jnp.float32)[:, None]
        farthest = float(usual[-1])
        at_far = count[:, hops : hops + 1]
        right_room = jnp.minimum(jnp.min(nominal - right_sums, axis=0, keepdims=True), farthest)
        left_room = jnp.minimum(jnp.min(nominal - left_sums, axis=0, keepdims=True), farthest)
        split = jnp.floor(jnp.sum(weigh * count, axis=1, keepdims=True) / (2.0 * hops))
        split = jnp.minimum(jnp.maximum(split, at_far - left_room), right_room)
        split = jnp.clip(split, 0.0, at_far)
        right_n = jnp.concatenate([right_sums + split, split], 0)
        left_n = jnp.concatenate([left_sums + at_far - split, at_far - split], 0)
        column = jnp.arange(chips)[:, None]
        before = ((kind < hops) & (column > kind) & (column < hops) & (kind > 0)) | (
            (kind > hops) & (column > hops) & (column < kind)
        )
        start = jnp.sum(count.reshape(chips, 1) * before, axis=0, keepdims=True)
        start = start + jnp.where((kind > 0) & (kind < hops), split, 0.0)
        start = start + jnp.where(kind > hops, at_far - split, 0.0)
        side = jnp.where(kind == 0, 2.0 * chip_rows, jnp.where(kind > hops, 1.0 * chip_rows, 0.0))
        slot = jnp.sum(marks_f * (start + side), axis=1, keepdims=True) + rank_in
        turned = marks[:, hops : hops + 1] & (rank_in >= split)
        slot = (slot + jnp.where(turned, chip_rows - split, 0.0)).astype(jnp.int32)[:, 0]

    with jax.named_scope("metadata"):
        item = jnp.arange(cap, dtype=jnp.int32)
        listed = jnp.sum(
            jnp.where(
                (rank_in[:, 0].astype(jnp.int32)[None, None, :] == item[None, :, None])
                & marks.T[:, None, :],
                local[None, None, :] + 1,
                0,
            ),
            axis=2,
        )
        far_kind = kind == hops
        right_start = jnp.where(far_kind, 0.0, start)
        right_end = jnp.where(far_kind, split, start + count)
        left_start = jnp.where(far_kind, -split, start)
        left_end = jnp.where(far_kind, at_far - split, start + count)
        most = jnp.maximum(right_n, left_n)
        head = jnp.concatenate(
            [right_start, right_end, left_start, left_end]
            + [jnp.broadcast_to(most[h : h + 1], (1, chips)) for h in range(hops)],
            0,
        ).astype(jnp.int32).T
        table = jnp.concatenate([head, listed], 1)
        lanes = table.shape[1]
        target = (place(jnp.arange(peers, dtype=jnp.int32) // 2) - here) % chips
        outgoing = jnp.sum(
            jnp.where((target[:, None] == jnp.arange(chips)[None, :])[:, :, None], table[None], 0),
            axis=1,
        )
        groups = lax.axis_size("groups")
        outgoing = jnp.broadcast_to(outgoing[None], (groups, peers, lanes)).reshape(-1, lanes)
        incoming = lax.all_to_all(
            outgoing, ("groups", "replica"), split_axis=0, concat_axis=0, tiled=True
        )
        needed = jnp.max(incoming[:, 4 : 4 + hops], axis=0, keepdims=True)
        overfull = jnp.any(needed > jnp.asarray([usual], jnp.int32))
        incoming = lax.dynamic_slice_in_dim(incoming, lax.axis_index("groups") * peers, peers, 0)
        source = place(jnp.arange(peers, dtype=jnp.int32) // 2)
        same_core = (jnp.arange(peers) % 2) == core
        back = (here - source) % chips
        chosen_source = (back[None, :] == jnp.arange(chips)[:, None]) & same_core[None, :]
        heard = jnp.sum(jnp.where(chosen_source[:, :, None], incoming[None], 0), axis=1)

    def exchange(tier, features, slot, heard, tokens, weight, down_factors, up_factors, own_scales):
        ways = (1, -1)
        far, second = tier[-1], tier[1]

        def packed(base, first, size):
            hit = (base + first + jnp.arange(size, dtype=jnp.int32))[:, None] == slot[None, :]
            return jnp.dot(
                hit.astype(jnp.bfloat16), features, preferred_element_type=jnp.float32
            ).astype(jnp.bfloat16)

        def part(direction, first, last):
            return packed(0 if direction > 0 else chip_rows, first, last - first)

        keys = [(d, b) for b in range(2) for d in ways]
        sent = [part(d, *((0, far) if b == 0 else (far, second))) for d, b in keys]
        with jax.named_scope("small_weights"):
            given_up = across(
                lax.dynamic_slice_in_dim(up_factors, (1 - core) * half_cols, half_cols, 2)
            )
            scales = jnp.concatenate([own_scales, across(own_scales)], 0)
        sent, (heard, given_up, scales) = tied(sent, [heard, given_up, scales])
        (tokens, weight, down_factors, up_factors), sent = tied(
            [tokens, weight, down_factors, up_factors], sent
        )
        arrived = {1: {k: around(v, k[0]) for k, v in zip(keys, sent)}}

        with jax.named_scope("weights"):
            given_down = across(lax.dynamic_slice_in_dim(down_factors, (1 - core) * half, half, 2))
            down = jnp.concatenate(
                [lax.dynamic_slice_in_dim(down_factors, core * half, half, 2), given_down], 0
            ).reshape(adapters * rank, half)
            up = jnp.concatenate(
                [lax.dynamic_slice_in_dim(up_factors, core * half_cols, half_cols, 2), given_up], 0
            ).reshape(adapters * rank, half_cols)
        base = jnp.dot(tokens, weight, preferred_element_type=jnp.float32)

        def labels(direction, h, first, size):
            row = heard[h if direction > 0 else chips - h]
            begin, end = (row[0], row[1]) if direction > 0 else (row[2], row[3])
            at = first + jnp.arange(size, dtype=jnp.int32)
            hit = (at - begin)[:, None] == item[None, :]
            label = jnp.sum(jnp.where(hit, row[4 + hops :][None, :], 0), axis=1) - 1
            return jnp.where(at < end, label, -1)

        def chosen_by(label):
            turned = jnp.where(core == 0, label, (label + own_adapters) % adapters)
            return (label >= 0)[:, None] & (turned[:, None] == jnp.arange(adapters)[None, :])

        def low_part(x, label):
            chosen = chosen_by(label)
            wide = lax.dot_general(
                x, down, (((1,), (1,)), ((), ())), preferred_element_type=jnp.float32
            )
            return jnp.sum(
                wide.reshape(x.shape[0], adapters, rank) * chosen.astype(jnp.float32)[:, :, None],
                axis=1,
            )

        def product(low, label):
            chosen = chosen_by(label)
            total = low + across(low)
            factor = jnp.sum(jnp.where(chosen, scales[None, :], 0.0), axis=1)
            scaled = (total * factor[:, None]).astype(jnp.bfloat16)
            spread = (scaled[:, None, :] * chosen.astype(jnp.bfloat16)[:, :, None]).reshape(
                -1, adapters * rank
            )
            return jnp.dot(spread, up, preferred_element_type=jnp.float32).astype(jnp.bfloat16)

        def hop_low(h, first, blocks):
            size = sum(v.shape[0] for v in blocks) // 2
            x = jnp.concatenate(blocks, 0)
            label = jnp.concatenate([labels(d, h, first, size) for d in ways], 0)
            return low_part(x, label), label, size

        def in_order(blocks):
            return [blocks[d, b] for d in ways for b in range(2) if (d, b) in blocks]

        own_label = heard[0, 4 + hops :] - 1
        own_low = low_part(packed(2 * chip_rows, 0, cap), own_label)
        lows = {}
        before = [base, own_low, down, up]
        late = {}
        for h in range(1, hops):
            keys = list(arrived[h])
            tie, values = tied(before, [arrived[h][k] for k in keys])
            if h == 1:
                base, own_low, down, up = tie
            else:
                lows[h - 1] = (tie[0],) + lows[h - 1][1:]
            blocks = dict(zip(keys, values))
            onward = {}
            for (d, b), v in blocks.items():
                v = v if b == 0 else v[: tier[h] - far]
                if v.shape[0] > 0:
                    onward[d, b] = around(v, d)
            arrived[h + 1] = onward
            if h == hops - 1 and tier[0] > second:
                (slot_late,), _ = tied([slot], values)
                slot, slot_now = slot_late, slot
                late = {(d, 0): around(part(d, second, tier[0]), d) for d in ways}
                slot = slot_now
            lows[h] = hop_low(h, 0, in_order(blocks))
            before = [lows[h][0]]
        lows[hops] = hop_low(hops, 0, in_order(arrived[hops]))
        back = None
        for h in range(hops, 0, -1):
            low, label, size = lows[h]
            delta = product(low, label)
            delta = [delta[:size], delta[size:]]
            if back is not None:
                delta = [
                    v + jnp.pad(b, ((0, v.shape[0] - b.shape[0]), (0, 0)))
                    for v, b in zip(delta, back)
                ]
            back = [around(v, -d) for v, d in zip(delta, ways)]
        results = [[b] for b in back]
        if late:
            low, label, size = hop_low(1, second, in_order(late))
            delta = product(low, label)
            results[0].append(around(delta[:size], -1))
            results[1].append(around(delta[size:], 1))
        own_delta = product(own_low, own_label)
        finished = jnp.concatenate(results[0] + results[1] + [own_delta], 0)
        column = jnp.where(
            slot < chip_rows,
            slot,
            jnp.where(slot < 2 * chip_rows, slot - chip_rows + tier[0], slot - 2 * chip_rows + 2 * tier[0]),
        )
        hit = (column[:, None] == jnp.arange(finished.shape[0], dtype=jnp.int32)[None, :]).astype(
            jnp.bfloat16
        )

        def taken(h):
            return jnp.dot(h, finished, preferred_element_type=jnp.float32).astype(jnp.bfloat16)

        given = across(taken(hit[rows:]))
        kept = taken(hit[:rows])
        delta = jnp.where(
            core == 0,
            jnp.concatenate([kept, given], 1),
            jnp.concatenate([given, kept], 1),
        )
        return (base + delta.astype(jnp.float32)).astype(jnp.bfloat16)

    given = (
        features,
        slot,
        heard,
        tokens,
        base_value_weight,
        down_factors,
        up_factors,
        adapter_scales,
    )

    values = exchange(usual, *given)
    return lax.cond(
        overfull,
        lambda kept, *rest: exchange(largest, *rest),
        lambda kept, *rest: kept,
        values,
        *given,
    )


def by_all_to_all(
    tokens, row_adapter_index, base_value_weight, down_factors, up_factors, adapter_scales
):
    peers = lax.axis_size("replica")
    input_rows = tokens.shape[0]
    feature_width = tokens.shape[1]
    rows_per_replica = down_factors.shape[0]
    rank_index = down_factors.shape[1]
    capacity = 3 * input_rows // peers
    slots = peers * capacity
    holder = row_adapter_index // rows_per_replica
    local_slot = row_adapter_index % rows_per_replica
    dest_table = (holder[:, None] == jnp.arange(peers, dtype=jnp.int32)[None, :]).astype(jnp.int32)
    position = jnp.sum(jnp.cumsum(dest_table, axis=0) * dest_table, axis=1) - 1
    target = holder * capacity + position
    outbox = jnp.zeros((slots, feature_width), tokens.dtype).at[target].set(tokens)
    labels = jnp.full((slots,), -1, jnp.int32).at[target].set(local_slot)
    inbox, in_labels = (
        lax.all_to_all(
            outbox.reshape(peers, capacity, feature_width),
            "replica",
            split_axis=0,
            concat_axis=0,
            tiled=True,
        ),
        lax.all_to_all(
            labels.reshape(peers, capacity), "replica", split_axis=0, concat_axis=0, tiled=True
        ),
    )
    received = inbox.reshape(slots, feature_width)
    marks = in_labels.reshape(slots)
    selected_adapters = (
        marks[:, None] == jnp.arange(rows_per_replica, dtype=jnp.int32)[None, :]
    ).astype(jnp.float32)
    stacked_down_factors = down_factors.reshape(rows_per_replica * rank_index, feature_width)
    wide = lax.dot_general(
        received, stacked_down_factors, (((1,), (1,)), ((), ())), preferred_element_type=jnp.float32
    )
    partial_low = jnp.sum(
        wide.reshape(slots, rows_per_replica, rank_index) * selected_adapters[:, :, None], axis=1
    )
    low_rank_output = lax.psum(partial_low, "tensor")
    scale_factor = jnp.sum(selected_adapters * adapter_scales[None, :], axis=1)
    scaled_output = (low_rank_output * scale_factor[:, None]).astype(jnp.bfloat16)
    spread_rows = (
        scaled_output[:, None, :] * selected_adapters[:, :, None].astype(jnp.bfloat16)
    ).reshape(slots, rows_per_replica * rank_index)
    delta = jnp.dot(
        spread_rows,
        up_factors.reshape(rows_per_replica * rank_index, up_factors.shape[2]),
        preferred_element_type=jnp.float32,
    )
    base_part = jnp.dot(received, base_value_weight, preferred_element_type=jnp.float32)
    base_cols = lax.psum_scatter(base_part, "tensor", scatter_dimension=1, tiled=True)
    finished = base_cols + delta
    returned = lax.all_to_all(
        finished.reshape(peers, capacity, finished.shape[1]).astype(jnp.bfloat16),
        "replica",
        split_axis=0,
        concat_axis=0,
        tiled=True,
    ).astype(jnp.float32)
    total = returned.reshape(slots, finished.shape[1])[target]
    return total.astype(jnp.bfloat16)


def solution(mesh):
    in_specs = (
        P(("groups", "replica"), "tensor"),
        P(("groups", "replica")),
        P("tensor", None),
        P("replica", None, "tensor"),
        P("replica", None, "tensor"),
        P("replica"),
    )
    out_specs = P(("groups", "replica"), "tensor")
    whole_rows = mesh.shape["tensor"] == 1 and mesh.shape["replica"] % 4 == 0
    return jax.shard_map(
        by_ring if whole_rows else by_all_to_all,
        mesh=mesh,
        in_specs=in_specs,
        out_specs=out_specs,
        check_vma=False,
    )
```

```python
import jax
import jax.numpy as jnp
from jax import lax
from jax.sharding import PartitionSpec as P


def sizes_for(rows, cap):
    chip_rows = 2 * rows
    unit = chip_rows // 32
    usual = tuple(unit * s for s in (23, 17, 12, 6))
    return usual, (chip_rows, chip_rows, min(chip_rows, 2 * cap), cap)


def tied(*groups):
    flat = [v for g in groups for v in g]
    flat = list(lax.optimization_barrier(tuple(flat)))
    out = []
    for g in groups:
        out.append(flat[: len(g)])
        flat = flat[len(g) :]
    return out


def by_ring(tokens, row_adapter_index, base_value_weight, down_factors, up_factors, adapter_scales):
    rows, width = tokens.shape
    own_adapters, rank, _ = down_factors.shape
    cols = base_value_weight.shape[1]
    half, half_cols = width // 2, cols // 2
    peers = lax.axis_size("replica")
    chips = peers // 2
    lines = chips // 2
    hops = chips // 2
    adapters = 2 * own_adapters
    chip_rows = 2 * rows
    cap = 4 * (3 * rows // peers)
    usual, largest = sizes_for(rows, cap)
    me = lax.axis_index("replica")
    core = me % 2
    order = [2 * z for z in range(lines)] + [2 * z + 1 for z in reversed(range(lines))]

    def place(c):
        return jnp.where(c % 2 == 0, c // 2, chips - 1 - c // 2)

    here = place(me // 2)

    def across(v):
        return lax.ppermute(v, "replica", [(i, i ^ 1) for i in range(peers)])

    def around(v, step):
        moves = [
            (2 * order[p] + c, 2 * order[(p + step) % chips] + c)
            for p in range(chips)
            for c in range(2)
        ]
        return lax.ppermute(v, "replica", moves)

    groups = lax.axis_size("groups")
    with jax.named_scope("indices"):
        other_index = across(row_adapter_index)
        outgoing = jnp.broadcast_to(row_adapter_index[None, :], (groups * peers, rows))
        every = lax.all_to_all(
            outgoing, ("groups", "replica"), split_axis=0, concat_axis=0, tiled=True
        ).reshape(groups * chips, chip_rows)

    with jax.named_scope("halves"):
        mine = lax.dynamic_slice_in_dim(tokens, core * half, half, 1)
        gone = lax.dynamic_slice_in_dim(tokens, (1 - core) * half, half, 1)
        features = jnp.concatenate([mine, across(gone)], 0)
        (down_late, up_late), _ = tied([down_factors, up_factors], [gone])
        given_down = across(lax.dynamic_slice_in_dim(down_late, (1 - core) * half, half, 2))
        given_up = across(
            lax.dynamic_slice_in_dim(up_late, (1 - core) * half_cols, half_cols, 2)
        )
        other_scales = across(adapter_scales)

    kind = jnp.arange(chips)[None, :]
    spot = jnp.arange(chip_rows, dtype=jnp.int32)
    earlier = (spot[None, :] < spot[:, None]).astype(jnp.bfloat16)

    def slots_of(index, position):
        distance = (place(index // adapters) - position) % chips
        marks = distance[:, :, None] == jnp.arange(chips)[None, None, :]
        ahead = jnp.einsum(
            "rs,gsk->grk", earlier, marks.astype(jnp.bfloat16), preferred_element_type=jnp.float32
        )
        marks_f = marks.astype(jnp.float32)
        rank_in = jnp.sum(ahead * marks_f, axis=2)
        count = jnp.sum(marks_f, axis=1)

        def over(mask):
            return jnp.sum(count * mask, axis=1, keepdims=True)

        right = [over((kind >= h) & (kind < hops)) for h in range(1, hops)]
        left = [over((kind > hops) & (kind <= chips - h)) for h in range(1, hops)]
        at_far = count[:, hops : hops + 1]
        right_room = jnp.full_like(at_far, usual[-1])
        left_room = right_room
        for h in range(1, hops):
            right_room = jnp.minimum(right_room, usual[h - 1] - right[h - 1])
            left_room = jnp.minimum(left_room, usual[h - 1] - left[h - 1])
        split = jnp.floor((sum(left) - sum(right) + hops * at_far) / (2.0 * hops))
        split = jnp.minimum(jnp.maximum(split, at_far - left_room), right_room)
        split = jnp.clip(split, 0.0, at_far)
        most = [jnp.maximum(r + split, l + at_far - split) for r, l in zip(right, left)]
        most = jnp.concatenate(most + [jnp.maximum(split, at_far - split)], 1)
        slot = rank_in + jnp.where(
            distance == 0,
            2.0 * chip_rows,
            jnp.where((distance == hops) & (rank_in >= split), chip_rows - split, 0.0),
        )
        for h in range(1, hops):
            beyond = right[h] if h + 1 < hops else 0.0
            slot = slot + jnp.where(distance == h, beyond + split, 0.0)
            beyond = left[h] if h + 1 < hops else 0.0
            slot = slot + jnp.where(distance == chips - h, beyond + at_far - split + chip_rows, 0.0)
        return slot.astype(jnp.int32), distance, most

    with jax.named_scope("own_slots"):
        both = jnp.where(
            core == 0,
            jnp.concatenate([row_adapter_index, other_index], 0),
            jnp.concatenate([other_index, row_adapter_index], 0),
        )
        slot = slots_of(both[None, :], here)[0][0]
        slot = jnp.where(core == 0, slot, jnp.roll(slot, rows))

    with jax.named_scope("all_slots"):
        positions = place(jnp.arange(groups * chips, dtype=jnp.int32) % chips)[:, None]
        all_slots, all_distances, most = slots_of(every, positions)
        overfull = jnp.any(most > jnp.asarray([usual], jnp.float32))

        def from_here(table):
            table = lax.dynamic_slice_in_dim(table, lax.axis_index("groups") * chips, chips, 0)
            ring = [table[c : c + 1] for c in order]
            return lax.dynamic_slice_in_dim(jnp.concatenate(ring + ring, 0), here, chips, 0)

        slots_here = from_here(all_slots)
        toward = (chips - jnp.arange(chips, dtype=jnp.int32))[:, None] % chips
        items_here = jnp.where(
            from_here(all_distances) == toward, from_here(every % adapters) + 1, 0
        )

    ways = (1, -1)

    def labels(side, line, first, size):
        at = side + first + jnp.arange(size, dtype=jnp.int32)
        hit = at[:, None] == slots_here[line][None, :]
        return jnp.sum(jnp.where(hit, items_here[line][None, :], 0), axis=1) - 1

    def chosen_by(label):
        turned = jnp.where(core == 0, label, (label + own_adapters) % adapters)
        return (label >= 0)[:, None] & (turned[:, None] == jnp.arange(adapters)[None, :])

    def packed(features, slot, base, first, size):
        hit = (base + first + jnp.arange(size, dtype=jnp.int32))[:, None] == slot[None, :]
        return jnp.dot(
            hit.astype(jnp.bfloat16), features, preferred_element_type=jnp.float32
        ).astype(jnp.bfloat16)

    def low_part(x, label, down):
        chosen = chosen_by(label)
        wide = lax.dot_general(
            x, down, (((1,), (1,)), ((), ())), preferred_element_type=jnp.float32
        )
        return jnp.sum(
            wide.reshape(x.shape[0], adapters, rank) * chosen.astype(jnp.float32)[:, :, None],
            axis=1,
        )

    def exchange(tier, features, slot, tokens, weight, down_own, down_other, up_own, up_other, scales):
        most_rows, second, third, far = tier

        def part(slot, first, last):
            return [
                packed(features, slot, 0 if d > 0 else chip_rows, first, last - first)
                for d in ways
            ]

        def onward(blocks, step=1):
            return [around(v, step * d) for v, d in zip(blocks, ways)]

        def label_of(h, first, size):
            return jnp.concatenate(
                [
                    labels(0, chips - h, first, size),
                    labels(chip_rows, h, first, size),
                ],
                0,
            )

        def low_of(h, first, blocks, down):
            label = label_of(h, first, blocks[0].shape[0])
            return low_part(jnp.concatenate(blocks, 0), label, down)

        def delta_of(low, label):
            chosen = chosen_by(label)
            total = low + across(low)
            factor = jnp.sum(jnp.where(chosen, scales[None, :], 0.0), axis=1)
            scaled = (total * factor[:, None]).astype(jnp.bfloat16)
            spread = (scaled[:, None, :] * chosen.astype(jnp.bfloat16)[:, :, None]).reshape(
                -1, adapters * rank
            )
            return jnp.dot(spread, up, preferred_element_type=jnp.float32).astype(jnp.bfloat16)

        def both_ways(low, h, first):
            size = low.shape[0] // 2
            delta = delta_of(low, label_of(h, first, size))
            return [delta[:size], delta[size:]]

        def added(small, large):
            return [
                b + jnp.pad(a, ((0, b.shape[0] - a.shape[0]), (0, 0)))
                for a, b in zip(small, large)
            ]

        sent = part(slot, 0, third)
        (tokens, weight, down_own, up_own, features), sent = tied(
            [tokens, weight, down_own, up_own, features], sent
        )
        first_hop = onward(sent)
        base = jnp.dot(tokens, weight, preferred_element_type=jnp.float32)
        down = jnp.concatenate(
            [lax.dynamic_slice_in_dim(down_own, core * half, half, 2), down_other], 0
        ).reshape(adapters * rank, half)
        up = jnp.concatenate(
            [lax.dynamic_slice_in_dim(up_own, core * half_cols, half_cols, 2), up_other], 0
        ).reshape(adapters * rank, half_cols)
        own_label = labels(2 * chip_rows, 0, 0, cap)
        own_low = low_part(packed(features, slot, 2 * chip_rows, 0, cap), own_label, down)
        (base, own_low, down, up), first_hop = tied([base, own_low, down, up], first_hop)
        second_hop = onward(first_hop)
        low_1 = low_of(1, 0, first_hop, down)
        near = part(slot, third, most_rows)
        (low_1, *near), second_hop = tied([low_1, *near], second_hop)
        third_hop = onward(second_hop)
        low_2 = low_of(2, 0, second_hop, down)
        (low_2,), third_hop = tied([low_2], third_hop)
        farthest, third_hop = tied([v[:far] for v in third_hop], third_hop)
        fourth_hop = onward(farthest)
        near_hop = onward(near)
        low_3 = low_of(3, 0, third_hop, down)
        (low_3,), fourth_hop = tied([low_3], fourth_hop)
        low_4 = low_of(4, 0, fourth_hop, down)
        (low_4,), near_hop = tied([low_4], near_hop)
        farther, near_hop = tied([v[: second - third] for v in near_hop], near_hop)
        near_second = onward(farther)
        low_near = low_of(1, third, near_hop, down)
        (low_near,), near_second = tied([low_near], near_second)
        low_near_2 = low_of(2, third, near_second, down)

        back = onward(both_ways(low_4, 4, 0), -1)
        for h, low in ((3, low_3), (2, low_2), (1, low_1)):
            back = onward(added(back, both_ways(low, h, 0)), -1)
        near_back = onward(both_ways(low_near, 1, third), -1)
        near_back = added(onward(both_ways(low_near_2, 2, third), -2), near_back)
        own_delta = delta_of(own_low, own_label)
        finished = jnp.concatenate(
            [back[0], near_back[0], back[1], near_back[1], own_delta], 0
        )
        column = jnp.where(
            slot < chip_rows,
            slot,
            jnp.where(
                slot < 2 * chip_rows,
                slot - chip_rows + most_rows,
                slot - 2 * chip_rows + 2 * most_rows,
            ),
        )
        hit = (column[:, None] == jnp.arange(finished.shape[0], dtype=jnp.int32)[None, :]).astype(
            jnp.bfloat16
        )

        def taken(h):
            return jnp.dot(h, finished, preferred_element_type=jnp.float32).astype(jnp.bfloat16)

        given = across(taken(hit[rows:]))
        kept = taken(hit[:rows])
        delta = jnp.where(
            core == 0,
            jnp.concatenate([kept, given], 1),
            jnp.concatenate([given, kept], 1),
        )
        return (base + delta.astype(jnp.float32)).astype(jnp.bfloat16)

    given = (
        lax.optimization_barrier(features),
        slot,
        tokens,
        base_value_weight,
        down_factors,
        given_down,
        up_factors,
        given_up,
        jnp.concatenate([adapter_scales, other_scales], 0),
    )
    values = exchange(usual, *given)
    return lax.cond(
        overfull,
        lambda kept, *rest: exchange(largest, *rest),
        lambda kept, *rest: kept,
        values,
        *given,
    )


def by_all_to_all(
    tokens, row_adapter_index, base_value_weight, down_factors, up_factors, adapter_scales
):
    peers = lax.axis_size("replica")
    input_rows = tokens.shape[0]
    feature_width = tokens.shape[1]
    rows_per_replica = down_factors.shape[0]
    rank_index = down_factors.shape[1]
    capacity = 3 * input_rows // peers
    slots = peers * capacity
    holder = row_adapter_index // rows_per_replica
    local_slot = row_adapter_index % rows_per_replica
    dest_table = (holder[:, None] == jnp.arange(peers, dtype=jnp.int32)[None, :]).astype(jnp.int32)
    position = jnp.sum(jnp.cumsum(dest_table, axis=0) * dest_table, axis=1) - 1
    target = holder * capacity + position
    outbox = jnp.zeros((slots, feature_width), tokens.dtype).at[target].set(tokens)
    labels = jnp.full((slots,), -1, jnp.int32).at[target].set(local_slot)
    inbox, in_labels = (
        lax.all_to_all(
            outbox.reshape(peers, capacity, feature_width),
            "replica",
            split_axis=0,
            concat_axis=0,
            tiled=True,
        ),
        lax.all_to_all(
            labels.reshape(peers, capacity), "replica", split_axis=0, concat_axis=0, tiled=True
        ),
    )
    received = inbox.reshape(slots, feature_width)
    marks = in_labels.reshape(slots)
    selected_adapters = (
        marks[:, None] == jnp.arange(rows_per_replica, dtype=jnp.int32)[None, :]
    ).astype(jnp.float32)
    stacked_down_factors = down_factors.reshape(rows_per_replica * rank_index, feature_width)
    wide = lax.dot_general(
        received, stacked_down_factors, (((1,), (1,)), ((), ())), preferred_element_type=jnp.float32
    )
    partial_low = jnp.sum(
        wide.reshape(slots, rows_per_replica, rank_index) * selected_adapters[:, :, None], axis=1
    )
    low_rank_output = lax.psum(partial_low, "tensor")
    scale_factor = jnp.sum(selected_adapters * adapter_scales[None, :], axis=1)
    scaled_output = (low_rank_output * scale_factor[:, None]).astype(jnp.bfloat16)
    spread_rows = (
        scaled_output[:, None, :] * selected_adapters[:, :, None].astype(jnp.bfloat16)
    ).reshape(slots, rows_per_replica * rank_index)
    delta = jnp.dot(
        spread_rows,
        up_factors.reshape(rows_per_replica * rank_index, up_factors.shape[2]),
        preferred_element_type=jnp.float32,
    )
    base_part = jnp.dot(received, base_value_weight, preferred_element_type=jnp.float32)
    base_cols = lax.psum_scatter(base_part, "tensor", scatter_dimension=1, tiled=True)
    finished = base_cols + delta
    returned = lax.all_to_all(
        finished.reshape(peers, capacity, finished.shape[1]).astype(jnp.bfloat16),
        "replica",
        split_axis=0,
        concat_axis=0,
        tiled=True,
    ).astype(jnp.float32)
    total = returned.reshape(slots, finished.shape[1])[target]
    return total.astype(jnp.bfloat16)


def solution(mesh):
    in_specs = (
        P(("groups", "replica"), "tensor"),
        P(("groups", "replica")),
        P("tensor", None),
        P("replica", None, "tensor"),
        P("replica", None, "tensor"),
        P("replica"),
    )
    out_specs = P(("groups", "replica"), "tensor")
    whole_rows = mesh.shape["tensor"] == 1 and mesh.shape["replica"] == 16
    return jax.shard_map(
        by_ring if whole_rows else by_all_to_all,
        mesh=mesh,
        in_specs=in_specs,
        out_specs=out_specs,
        check_vma=False,
    )
```

```python
import jax
import jax.numpy as jnp
from jax import lax
from jax.sharding import PartitionSpec as P


def sizes_for(rows, cap):
    chip_rows = 2 * rows
    unit = chip_rows // 32
    usual = tuple(unit * s for s in (23, 18, 12, 6))
    return usual, (chip_rows, chip_rows, min(chip_rows, 2 * cap), cap)


def tied(*groups):
    flat = [v for g in groups for v in g]
    flat = list(lax.optimization_barrier(tuple(flat)))
    out = []
    for g in groups:
        out.append(flat[: len(g)])
        flat = flat[len(g) :]
    return out


def by_ring(tokens, row_adapter_index, base_value_weight, down_factors, up_factors, adapter_scales):
    rows, width = tokens.shape
    own_adapters, rank, _ = down_factors.shape
    cols = base_value_weight.shape[1]
    half, half_cols = width // 2, cols // 2
    peers = lax.axis_size("replica")
    chips = peers // 2
    lines = chips // 2
    hops = chips // 2
    adapters = 2 * own_adapters
    chip_rows = 2 * rows
    cap = 4 * (3 * rows // peers)
    usual, largest = sizes_for(rows, cap)
    me = lax.axis_index("replica")
    core = me % 2
    order = [2 * z for z in range(lines)] + [2 * z + 1 for z in reversed(range(lines))]

    def place(c):
        return jnp.where(c % 2 == 0, c // 2, chips - 1 - c // 2)

    here = place(me // 2)

    def across(v):
        return lax.ppermute(v, "replica", [(i, i ^ 1) for i in range(peers)])

    def around(v, step):
        moves = [
            (2 * order[p] + c, 2 * order[(p + step) % chips] + c)
            for p in range(chips)
            for c in range(2)
        ]
        return lax.ppermute(v, "replica", moves)

    groups = lax.axis_size("groups")
    with jax.named_scope("other_core"):
        other_tokens = across(tokens)
        other_scales = across(adapter_scales)
        up_other = across(up_factors)
        down_other = across(down_factors)

    with jax.named_scope("indices"):
        outgoing = jnp.broadcast_to(row_adapter_index[None, :], (groups * peers, rows))
        every = lax.all_to_all(
            outgoing, ("groups", "replica"), split_axis=0, concat_axis=0, tiled=True
        ).reshape(groups * chips, chip_rows)

    def half_of(v, axis):
        size = v.shape[axis] // 2
        return lax.dynamic_slice_in_dim(v, core * size, size, axis)

    features = jnp.concatenate([half_of(tokens, 1), half_of(other_tokens, 1)], 0)

    kind = jnp.arange(chips)[None, :]
    spot = jnp.arange(chip_rows, dtype=jnp.int32)
    earlier = (spot[None, :] < spot[:, None]).astype(jnp.bfloat16)

    def slots_of(index, position):
        distance = (place(index // adapters) - position) % chips
        marks = distance[:, :, None] == jnp.arange(chips)[None, None, :]
        ahead = jnp.einsum(
            "rs,gsk->grk", earlier, marks.astype(jnp.bfloat16), preferred_element_type=jnp.float32
        )
        marks_f = marks.astype(jnp.float32)
        rank_in = jnp.sum(ahead * marks_f, axis=2)
        count = jnp.sum(marks_f, axis=1)

        def over(mask):
            return jnp.sum(count * mask, axis=1, keepdims=True)

        right = [over((kind >= h) & (kind < hops)) for h in range(1, hops)]
        left = [over((kind > hops) & (kind <= chips - h)) for h in range(1, hops)]
        at_far = count[:, hops : hops + 1]
        right_room = jnp.full_like(at_far, usual[-1])
        left_room = right_room
        for h in range(1, hops):
            right_room = jnp.minimum(right_room, usual[h - 1] - right[h - 1])
            left_room = jnp.minimum(left_room, usual[h - 1] - left[h - 1])
        split = jnp.floor((sum(left) - sum(right) + hops * at_far) / (2.0 * hops))
        split = jnp.minimum(jnp.maximum(split, at_far - left_room), right_room)
        split = jnp.clip(split, 0.0, at_far)
        most = [jnp.maximum(r + split, l + at_far - split) for r, l in zip(right, left)]
        most = jnp.concatenate(most + [jnp.maximum(split, at_far - split)], 1)
        slot = rank_in + jnp.where(
            distance == 0,
            2.0 * chip_rows,
            jnp.where((distance == hops) & (rank_in >= split), chip_rows - split, 0.0),
        )
        for h in range(1, hops):
            beyond = right[h] if h + 1 < hops else 0.0
            slot = slot + jnp.where(distance == h, beyond + split, 0.0)
            beyond = left[h] if h + 1 < hops else 0.0
            slot = slot + jnp.where(distance == chips - h, beyond + at_far - split + chip_rows, 0.0)
        return slot.astype(jnp.int32), distance, most

    with jax.named_scope("all_slots"):
        positions = place(jnp.arange(groups * chips, dtype=jnp.int32) % chips)[:, None]
        all_slots, all_distances, most = slots_of(every, positions)
        overfull = jnp.any(most > jnp.asarray([usual], jnp.float32))

        def from_here(table):
            table = lax.dynamic_slice_in_dim(table, lax.axis_index("groups") * chips, chips, 0)
            ring = [table[c : c + 1] for c in order]
            return lax.dynamic_slice_in_dim(jnp.concatenate(ring + ring, 0), here, chips, 0)

        slots_here = from_here(all_slots)
        slot = jnp.where(core == 0, slots_here[0], jnp.roll(slots_here[0], rows))
        toward = (chips - jnp.arange(chips, dtype=jnp.int32))[:, None] % chips
        items_here = jnp.where(
            from_here(all_distances) == toward, from_here(every % adapters) + 1, 0
        )

    ways = (1, -1)

    def labels(tables, side, line, first, size):
        slots_here, items_here = tables
        at = side + first + jnp.arange(size, dtype=jnp.int32)
        hit = at[:, None] == slots_here[line][None, :]
        return jnp.sum(jnp.where(hit, items_here[line][None, :], 0), axis=1) - 1

    def chosen_by(label):
        turned = jnp.where(core == 0, label, (label + own_adapters) % adapters)
        return (label >= 0)[:, None] & (turned[:, None] == jnp.arange(adapters)[None, :])

    def packed(features, slot, base, first, size):
        hit = (base + first + jnp.arange(size, dtype=jnp.int32))[:, None] == slot[None, :]
        return jnp.dot(
            hit.astype(jnp.bfloat16), features, preferred_element_type=jnp.float32
        ).astype(jnp.bfloat16)

    def low_part(x, label, down):
        chosen = chosen_by(label)
        wide = lax.dot_general(
            x, down, (((1,), (1,)), ((), ())), preferred_element_type=jnp.float32
        )
        return jnp.sum(
            wide.reshape(x.shape[0], adapters, rank) * chosen.astype(jnp.float32)[:, :, None],
            axis=1,
        )

    def exchange(tier, features, slot, slots_here, items_here, tokens, weight, down_own, down_other, up_own, up_other, scales):
        most_rows, second, third, far = tier

        def part(slot, first, last):
            return [
                packed(features, slot, 0 if d > 0 else chip_rows, first, last - first)
                for d in ways
            ]

        def onward(blocks, step=1):
            return [around(v, step * d) for v, d in zip(blocks, ways)]

        def label_of(h, first, size):
            return jnp.concatenate(
                [
                    labels(tables, 0, chips - h, first, size),
                    labels(tables, chip_rows, h, first, size),
                ],
                0,
            )

        def low_of(h, first, blocks, down):
            label = label_of(h, first, blocks[0].shape[0])
            return low_part(jnp.concatenate(blocks, 0), label, down)

        def delta_of(low, label):
            chosen = chosen_by(label)
            total = low + across(low)
            factor = jnp.sum(jnp.where(chosen, scales[None, :], 0.0), axis=1)
            scaled = (total * factor[:, None]).astype(jnp.bfloat16)
            spread = (scaled[:, None, :] * chosen.astype(jnp.bfloat16)[:, :, None]).reshape(
                -1, adapters * rank
            )
            return jnp.dot(spread, up, preferred_element_type=jnp.float32).astype(jnp.bfloat16)

        def both_ways(low, h, first):
            size = low.shape[0] // 2
            delta = delta_of(low, label_of(h, first, size))
            return [delta[:size], delta[size:]]

        def added(small, large):
            return [
                b + jnp.pad(a, ((0, b.shape[0] - a.shape[0]), (0, 0)))
                for a, b in zip(small, large)
            ]

        sent = part(slot, 0, third)
        (down_own, up_own, slot_late), sent = tied([down_own, up_own, slot], sent)
        first_hop = onward(sent)
        down = jnp.concatenate([half_of(down_own, 2), half_of(down_other, 2)], 0)
        down = down.reshape(adapters * rank, half)
        up = jnp.concatenate([half_of(up_own, 2), half_of(up_other, 2)], 0)
        up = up.reshape(adapters * rank, half_cols)
        near = part(slot_late, third, most_rows)
        own_rows = packed(features, slot_late, 2 * chip_rows, 0, cap)
        tables = (slots_here, items_here)
        (tokens, down, up, own_rows, *near), first_hop, tables = tied(
            [tokens, down, up, own_rows, *near], first_hop, tables
        )
        second_hop = onward(first_hop)
        low_1 = low_of(1, 0, first_hop, down)
        base = jnp.dot(tokens, weight, preferred_element_type=jnp.float32)
        (low_1, base, own_rows), second_hop = tied([low_1, base, own_rows], second_hop)
        third_hop = onward(second_hop)
        low_2 = low_of(2, 0, second_hop, down)
        own_label = labels(tables, 2 * chip_rows, 0, 0, cap)
        own_low = low_part(own_rows, own_label, down)
        (low_2, own_low, *near), third_hop = tied([low_2, own_low, *near], third_hop)
        farthest, third_hop = tied([v[:far] for v in third_hop], third_hop)
        fourth_hop = onward(farthest)
        near_hop = onward(near)
        low_3 = low_of(3, 0, third_hop, down)
        (low_3,), fourth_hop = tied([low_3], fourth_hop)
        low_4 = low_of(4, 0, fourth_hop, down)
        result_4 = both_ways(low_4, 4, 0)
        result_4, near_hop = tied(result_4, near_hop)
        back = onward(result_4, -1)
        farther, near_hop = tied([v[: second - third] for v in near_hop], near_hop)
        near_second = onward(farther)
        low_near = low_of(1, third, near_hop, down)
        (low_near,), near_second = tied([low_near], near_second)
        low_near_2 = low_of(2, third, near_second, down)

        for h, low in ((3, low_3), (2, low_2), (1, low_1)):
            back = onward(added(back, both_ways(low, h, 0)), -1)
        near_back = onward(both_ways(low_near, 1, third), -1)
        near_back = added(onward(both_ways(low_near_2, 2, third), -2), near_back)
        own_delta = delta_of(own_low, own_label)
        finished = jnp.concatenate(
            [back[0], near_back[0], back[1], near_back[1], own_delta], 0
        )
        column = jnp.where(
            slot < chip_rows,
            slot,
            jnp.where(
                slot < 2 * chip_rows,
                slot - chip_rows + most_rows,
                slot - 2 * chip_rows + 2 * most_rows,
            ),
        )
        hit = (column[:, None] == jnp.arange(finished.shape[0], dtype=jnp.int32)[None, :]).astype(
            jnp.bfloat16
        )

        def taken(h):
            return jnp.dot(h, finished, preferred_element_type=jnp.float32).astype(jnp.bfloat16)

        given = across(taken(hit[rows:]))
        kept = taken(hit[:rows])
        delta = jnp.where(
            core == 0,
            jnp.concatenate([kept, given], 1),
            jnp.concatenate([given, kept], 1),
        )
        return (base + delta.astype(jnp.float32)).astype(jnp.bfloat16)

    given = (
        lax.optimization_barrier(features),
        slot,
        slots_here,
        items_here,
        tokens,
        base_value_weight,
        down_factors,
        down_other,
        up_factors,
        up_other,
        jnp.concatenate([adapter_scales, other_scales], 0),
    )
    values = exchange(usual, *given)
    return lax.cond(
        overfull,
        lambda kept, *rest: exchange(largest, *rest),
        lambda kept, *rest: kept,
        values,
        *given,
    )


def by_all_to_all(
    tokens, row_adapter_index, base_value_weight, down_factors, up_factors, adapter_scales
):
    peers = lax.axis_size("replica")
    input_rows = tokens.shape[0]
    feature_width = tokens.shape[1]
    rows_per_replica = down_factors.shape[0]
    rank_index = down_factors.shape[1]
    capacity = 3 * input_rows // peers
    slots = peers * capacity
    holder = row_adapter_index // rows_per_replica
    local_slot = row_adapter_index % rows_per_replica
    dest_table = (holder[:, None] == jnp.arange(peers, dtype=jnp.int32)[None, :]).astype(jnp.int32)
    position = jnp.sum(jnp.cumsum(dest_table, axis=0) * dest_table, axis=1) - 1
    target = holder * capacity + position
    outbox = jnp.zeros((slots, feature_width), tokens.dtype).at[target].set(tokens)
    labels = jnp.full((slots,), -1, jnp.int32).at[target].set(local_slot)
    inbox, in_labels = (
        lax.all_to_all(
            outbox.reshape(peers, capacity, feature_width),
            "replica",
            split_axis=0,
            concat_axis=0,
            tiled=True,
        ),
        lax.all_to_all(
            labels.reshape(peers, capacity), "replica", split_axis=0, concat_axis=0, tiled=True
        ),
    )
    received = inbox.reshape(slots, feature_width)
    marks = in_labels.reshape(slots)
    selected_adapters = (
        marks[:, None] == jnp.arange(rows_per_replica, dtype=jnp.int32)[None, :]
    ).astype(jnp.float32)
    stacked_down_factors = down_factors.reshape(rows_per_replica * rank_index, feature_width)
    wide = lax.dot_general(
        received, stacked_down_factors, (((1,), (1,)), ((), ())), preferred_element_type=jnp.float32
    )
    partial_low = jnp.sum(
        wide.reshape(slots, rows_per_replica, rank_index) * selected_adapters[:, :, None], axis=1
    )
    low_rank_output = lax.psum(partial_low, "tensor")
    scale_factor = jnp.sum(selected_adapters * adapter_scales[None, :], axis=1)
    scaled_output = (low_rank_output * scale_factor[:, None]).astype(jnp.bfloat16)
    spread_rows = (
        scaled_output[:, None, :] * selected_adapters[:, :, None].astype(jnp.bfloat16)
    ).reshape(slots, rows_per_replica * rank_index)
    delta = jnp.dot(
        spread_rows,
        up_factors.reshape(rows_per_replica * rank_index, up_factors.shape[2]),
        preferred_element_type=jnp.float32,
    )
    base_part = jnp.dot(received, base_value_weight, preferred_element_type=jnp.float32)
    base_cols = lax.psum_scatter(base_part, "tensor", scatter_dimension=1, tiled=True)
    finished = base_cols + delta
    returned = lax.all_to_all(
        finished.reshape(peers, capacity, finished.shape[1]).astype(jnp.bfloat16),
        "replica",
        split_axis=0,
        concat_axis=0,
        tiled=True,
    ).astype(jnp.float32)
    total = returned.reshape(slots, finished.shape[1])[target]
    return total.astype(jnp.bfloat16)


def solution(mesh):
    in_specs = (
        P(("groups", "replica"), "tensor"),
        P(("groups", "replica")),
        P("tensor", None),
        P("replica", None, "tensor"),
        P("replica", None, "tensor"),
        P("replica"),
    )
    out_specs = P(("groups", "replica"), "tensor")
    whole_rows = mesh.shape["tensor"] == 1 and mesh.shape["replica"] == 16
    return jax.shard_map(
        by_ring if whole_rows else by_all_to_all,
        mesh=mesh,
        in_specs=in_specs,
        out_specs=out_specs,
        check_vma=False,
    )
```

```python
import jax
import jax.numpy as jnp
from jax import lax
from jax.sharding import PartitionSpec as P


def sizes_for(rows, cap):
    chip_rows = 2 * rows
    unit = chip_rows // 32
    usual = tuple(unit * s for s in (23, 18, 12, 6))
    return usual, (chip_rows, chip_rows, min(chip_rows, 2 * cap), cap)


def tied(*groups):
    flat = [v for g in groups for v in g]
    flat = list(lax.optimization_barrier(tuple(flat)))
    out = []
    for g in groups:
        out.append(flat[: len(g)])
        flat = flat[len(g) :]
    return out


def by_ring(tokens, row_adapter_index, base_value_weight, down_factors, up_factors, adapter_scales):
    rows, width = tokens.shape
    own_adapters, rank, _ = down_factors.shape
    cols = base_value_weight.shape[1]
    half, half_cols = width // 2, cols // 2
    peers = lax.axis_size("replica")
    chips = peers // 2
    lines = chips // 2
    hops = chips // 2
    adapters = 2 * own_adapters
    chip_rows = 2 * rows
    cap = 4 * (3 * rows // peers)
    usual, largest = sizes_for(rows, cap)
    me = lax.axis_index("replica")
    core = me % 2
    order = [2 * z for z in range(lines)] + [2 * z + 1 for z in reversed(range(lines))]

    def place(c):
        return jnp.where(c % 2 == 0, c // 2, chips - 1 - c // 2)

    here = place(me // 2)

    def across(v):
        return lax.ppermute(v, "replica", [(i, i ^ 1) for i in range(peers)])

    def around(v, step):
        moves = [
            (2 * order[p] + c, 2 * order[(p + step) % chips] + c)
            for p in range(chips)
            for c in range(2)
        ]
        return lax.ppermute(v, "replica", moves)

    groups = lax.axis_size("groups")
    with jax.named_scope("other_core"):
        other_tokens = across(tokens)
        other_scales = across(adapter_scales)
        up_other = across(up_factors)
        (down_late,), (other_tokens, other_scales, up_other) = tied(
            [down_factors], [other_tokens, other_scales, up_other]
        )
        down_other = across(down_late)

    with jax.named_scope("indices"):
        outgoing = jnp.broadcast_to(row_adapter_index[None, :], (groups * peers, rows))
        every = lax.all_to_all(
            outgoing, ("groups", "replica"), split_axis=0, concat_axis=0, tiled=True
        ).reshape(groups * chips, chip_rows)

    def half_of(v, axis):
        size = v.shape[axis] // 2
        return lax.dynamic_slice_in_dim(v, core * size, size, axis)

    features = jnp.concatenate([half_of(tokens, 1), half_of(other_tokens, 1)], 0)

    kind = jnp.arange(chips)[None, :]
    spot = jnp.arange(chip_rows, dtype=jnp.int32)
    earlier = (spot[None, :] < spot[:, None]).astype(jnp.bfloat16)

    def slots_of(index, position):
        distance = (place(index // adapters) - position) % chips
        marks = distance[:, :, None] == jnp.arange(chips)[None, None, :]
        ahead = jnp.einsum(
            "rs,gsk->grk", earlier, marks.astype(jnp.bfloat16), preferred_element_type=jnp.float32
        )
        marks_f = marks.astype(jnp.float32)
        rank_in = jnp.sum(ahead * marks_f, axis=2)
        count = jnp.sum(marks_f, axis=1)

        def over(mask):
            return jnp.sum(count * mask, axis=1, keepdims=True)

        right = [over((kind >= h) & (kind < hops)) for h in range(1, hops)]
        left = [over((kind > hops) & (kind <= chips - h)) for h in range(1, hops)]
        at_far = count[:, hops : hops + 1]
        right_room = jnp.full_like(at_far, usual[-1])
        left_room = right_room
        for h in range(1, hops):
            right_room = jnp.minimum(right_room, usual[h - 1] - right[h - 1])
            left_room = jnp.minimum(left_room, usual[h - 1] - left[h - 1])
        split = jnp.floor((sum(left) - sum(right) + hops * at_far) / (2.0 * hops))
        split = jnp.minimum(jnp.maximum(split, at_far - left_room), right_room)
        split = jnp.clip(split, 0.0, at_far)
        most = [jnp.maximum(r + split, l + at_far - split) for r, l in zip(right, left)]
        most = jnp.concatenate(most + [jnp.maximum(split, at_far - split)], 1)
        slot = rank_in + jnp.where(
            distance == 0,
            2.0 * chip_rows,
            jnp.where((distance == hops) & (rank_in >= split), chip_rows - split, 0.0),
        )
        for h in range(1, hops):
            beyond = right[h] if h + 1 < hops else 0.0
            slot = slot + jnp.where(distance == h, beyond + split, 0.0)
            beyond = left[h] if h + 1 < hops else 0.0
            slot = slot + jnp.where(distance == chips - h, beyond + at_far - split + chip_rows, 0.0)
        return slot.astype(jnp.int32), distance, most

    with jax.named_scope("all_slots"):
        positions = place(jnp.arange(groups * chips, dtype=jnp.int32) % chips)[:, None]
        all_slots, all_distances, most = slots_of(every, positions)
        overfull = jnp.any(most > jnp.asarray([usual], jnp.float32))

        def from_here(table):
            table = lax.dynamic_slice_in_dim(table, lax.axis_index("groups") * chips, chips, 0)
            ring = [table[c : c + 1] for c in order]
            return lax.dynamic_slice_in_dim(jnp.concatenate(ring + ring, 0), here, chips, 0)

        slots_here = from_here(all_slots)
        slot = jnp.where(core == 0, slots_here[0], jnp.roll(slots_here[0], rows))
        toward = (chips - jnp.arange(chips, dtype=jnp.int32))[:, None] % chips
        items_here = jnp.where(
            from_here(all_distances) == toward, from_here(every % adapters) + 1, 0
        )

    ways = (1, -1)

    def labels(tables, side, line, first, size):
        slots_here, items_here = tables
        at = side + first + jnp.arange(size, dtype=jnp.int32)
        hit = at[:, None] == slots_here[line][None, :]
        return jnp.sum(jnp.where(hit, items_here[line][None, :], 0), axis=1) - 1

    def chosen_by(label):
        turned = jnp.where(core == 0, label, (label + own_adapters) % adapters)
        return (label >= 0)[:, None] & (turned[:, None] == jnp.arange(adapters)[None, :])

    def packed(features, slot, base, first, size):
        hit = (base + first + jnp.arange(size, dtype=jnp.int32))[:, None] == slot[None, :]
        return jnp.dot(
            hit.astype(jnp.bfloat16), features, preferred_element_type=jnp.float32
        ).astype(jnp.bfloat16)

    def low_part(x, label, down):
        chosen = chosen_by(label)
        wide = lax.dot_general(
            x, down, (((1,), (1,)), ((), ())), preferred_element_type=jnp.float32
        )
        return jnp.sum(
            wide.reshape(x.shape[0], adapters, rank) * chosen.astype(jnp.float32)[:, :, None],
            axis=1,
        )

    def exchange(tier, features, slot, slots_here, items_here, tokens, weight, down_own, down_other, up_own, up_other, scales):
        most_rows, second, third, far = tier

        def part(slot, first, last):
            return [
                packed(features, slot, 0 if d > 0 else chip_rows, first, last - first)
                for d in ways
            ]

        def onward(blocks, step=1):
            return [around(v, step * d) for v, d in zip(blocks, ways)]

        def label_of(h, first, size):
            return jnp.concatenate(
                [
                    labels(tables, 0, chips - h, first, size),
                    labels(tables, chip_rows, h, first, size),
                ],
                0,
            )

        def low_of(h, first, blocks, down):
            label = label_of(h, first, blocks[0].shape[0])
            return low_part(jnp.concatenate(blocks, 0), label, down)

        def delta_of(low, label):
            chosen = chosen_by(label)
            total = low + across(low)
            factor = jnp.sum(jnp.where(chosen, scales[None, :], 0.0), axis=1)
            scaled = (total * factor[:, None]).astype(jnp.bfloat16)
            spread = (scaled[:, None, :] * chosen.astype(jnp.bfloat16)[:, :, None]).reshape(
                -1, adapters * rank
            )
            return jnp.dot(spread, up, preferred_element_type=jnp.float32).astype(jnp.bfloat16)

        def both_ways(low, h, first):
            size = low.shape[0] // 2
            delta = delta_of(low, label_of(h, first, size))
            return [delta[:size], delta[size:]]

        def added(small, large):
            return [
                b + jnp.pad(a, ((0, b.shape[0] - a.shape[0]), (0, 0)))
                for a, b in zip(small, large)
            ]

        sent = part(slot, 0, third)
        (down_own, up_own, slot_late), sent = tied([down_own, up_own, slot], sent)
        first_hop = onward(sent)
        down = jnp.concatenate([half_of(down_own, 2), half_of(down_other, 2)], 0)
        down = down.reshape(adapters * rank, half)
        up = jnp.concatenate([half_of(up_own, 2), half_of(up_other, 2)], 0)
        up = up.reshape(adapters * rank, half_cols)
        near = part(slot_late, third, most_rows)
        own_rows = packed(features, slot_late, 2 * chip_rows, 0, cap)
        tables, (own_rows,) = tied([slots_here, items_here], [own_rows])
        own_label = labels(tables, 2 * chip_rows, 0, 0, cap)
        (tokens, down, up, own_rows, *near), first_hop = tied(
            [tokens, down, up, own_rows, *near], first_hop
        )
        second_hop = onward(first_hop)
        near_hop = onward(near)
        low_1 = low_of(1, 0, first_hop, down)
        own_low = low_part(own_rows, own_label, down)
        base = jnp.dot(tokens, weight, preferred_element_type=jnp.float32)
        (low_1, own_low, base), second_hop = tied([low_1, own_low, base], second_hop)
        third_hop = onward(second_hop)
        low_2 = low_of(2, 0, second_hop, down)
        (low_2,), near_hop = tied([low_2], near_hop)
        farther, near_hop = tied([v[: second - third] for v in near_hop], near_hop)
        near_second = onward(farther)
        low_near = low_of(1, third, near_hop, down)
        (low_near,), third_hop = tied([low_near], third_hop)
        farthest, third_hop = tied([v[:far] for v in third_hop], third_hop)
        fourth_hop = onward(farthest)
        low_3 = low_of(3, 0, third_hop, down)
        back = onward(both_ways(low_3, 3, 0), -1)
        (low_3,), near_second = tied([low_3], near_second)
        low_near_2 = low_of(2, third, near_second, down)
        (low_near_2,), fourth_hop = tied([low_near_2], fourth_hop)
        low_4 = low_of(4, 0, fourth_hop, down)
        far_back = onward(both_ways(low_4, 4, 0), -4)
        for h, low in ((2, low_2), (1, low_1)):
            back = onward(added(back, both_ways(low, h, 0)), -1)
        near_back = onward(both_ways(low_near, 1, third), -1)
        near_back = added(onward(both_ways(low_near_2, 2, third), -2), near_back)
        back = added(far_back, back)
        own_delta = delta_of(own_low, own_label)
        finished = jnp.concatenate(
            [back[0], near_back[0], back[1], near_back[1], own_delta], 0
        )
        column = jnp.where(
            slot < chip_rows,
            slot,
            jnp.where(
                slot < 2 * chip_rows,
                slot - chip_rows + most_rows,
                slot - 2 * chip_rows + 2 * most_rows,
            ),
        )
        hit = (column[:, None] == jnp.arange(finished.shape[0], dtype=jnp.int32)[None, :]).astype(
            jnp.bfloat16
        )

        def taken(h):
            return jnp.dot(h, finished, preferred_element_type=jnp.float32).astype(jnp.bfloat16)

        given = across(taken(hit[rows:]))
        kept = taken(hit[:rows])
        delta = jnp.where(
            core == 0,
            jnp.concatenate([kept, given], 1),
            jnp.concatenate([given, kept], 1),
        )
        return (base + delta.astype(jnp.float32)).astype(jnp.bfloat16)

    given = (
        lax.optimization_barrier(features),
        slot,
        slots_here,
        items_here,
        tokens,
        base_value_weight,
        down_factors,
        down_other,
        up_factors,
        up_other,
        jnp.concatenate([adapter_scales, other_scales], 0),
    )
    values = exchange(usual, *given)
    return lax.cond(
        overfull,
        lambda kept, *rest: exchange(largest, *rest),
        lambda kept, *rest: kept,
        values,
        *given,
    )


def by_all_to_all(
    tokens, row_adapter_index, base_value_weight, down_factors, up_factors, adapter_scales
):
    peers = lax.axis_size("replica")
    input_rows = tokens.shape[0]
    feature_width = tokens.shape[1]
    rows_per_replica = down_factors.shape[0]
    rank_index = down_factors.shape[1]
    capacity = 3 * input_rows // peers
    slots = peers * capacity
    holder = row_adapter_index // rows_per_replica
    local_slot = row_adapter_index % rows_per_replica
    dest_table = (holder[:, None] == jnp.arange(peers, dtype=jnp.int32)[None, :]).astype(jnp.int32)
    position = jnp.sum(jnp.cumsum(dest_table, axis=0) * dest_table, axis=1) - 1
    target = holder * capacity + position
    outbox = jnp.zeros((slots, feature_width), tokens.dtype).at[target].set(tokens)
    labels = jnp.full((slots,), -1, jnp.int32).at[target].set(local_slot)
    inbox, in_labels = (
        lax.all_to_all(
            outbox.reshape(peers, capacity, feature_width),
            "replica",
            split_axis=0,
            concat_axis=0,
            tiled=True,
        ),
        lax.all_to_all(
            labels.reshape(peers, capacity), "replica", split_axis=0, concat_axis=0, tiled=True
        ),
    )
    received = inbox.reshape(slots, feature_width)
    marks = in_labels.reshape(slots)
    selected_adapters = (
        marks[:, None] == jnp.arange(rows_per_replica, dtype=jnp.int32)[None, :]
    ).astype(jnp.float32)
    stacked_down_factors = down_factors.reshape(rows_per_replica * rank_index, feature_width)
    wide = lax.dot_general(
        received, stacked_down_factors, (((1,), (1,)), ((), ())), preferred_element_type=jnp.float32
    )
    partial_low = jnp.sum(
        wide.reshape(slots, rows_per_replica, rank_index) * selected_adapters[:, :, None], axis=1
    )
    low_rank_output = lax.psum(partial_low, "tensor")
    scale_factor = jnp.sum(selected_adapters * adapter_scales[None, :], axis=1)
    scaled_output = (low_rank_output * scale_factor[:, None]).astype(jnp.bfloat16)
    spread_rows = (
        scaled_output[:, None, :] * selected_adapters[:, :, None].astype(jnp.bfloat16)
    ).reshape(slots, rows_per_replica * rank_index)
    delta = jnp.dot(
        spread_rows,
        up_factors.reshape(rows_per_replica * rank_index, up_factors.shape[2]),
        preferred_element_type=jnp.float32,
    )
    base_part = jnp.dot(received, base_value_weight, preferred_element_type=jnp.float32)
    base_cols = lax.psum_scatter(base_part, "tensor", scatter_dimension=1, tiled=True)
    finished = base_cols + delta
    returned = lax.all_to_all(
        finished.reshape(peers, capacity, finished.shape[1]).astype(jnp.bfloat16),
        "replica",
        split_axis=0,
        concat_axis=0,
        tiled=True,
    ).astype(jnp.float32)
    total = returned.reshape(slots, finished.shape[1])[target]
    return total.astype(jnp.bfloat16)


def solution(mesh):
    in_specs = (
        P(("groups", "replica"), "tensor"),
        P(("groups", "replica")),
        P("tensor", None),
        P("replica", None, "tensor"),
        P("replica", None, "tensor"),
        P("replica"),
    )
    out_specs = P(("groups", "replica"), "tensor")
    whole_rows = mesh.shape["tensor"] == 1 and mesh.shape["replica"] == 16
    return jax.shard_map(
        by_ring if whole_rows else by_all_to_all,
        mesh=mesh,
        in_specs=in_specs,
        out_specs=out_specs,
        check_vma=False,
    )
```

```python
import jax
import jax.numpy as jnp
from jax import lax
from jax.sharding import PartitionSpec as P


def sizes_for(rows, cap):
    chip_rows = 2 * rows
    unit = chip_rows // 32
    usual = tuple(unit * s for s in (23, 18, 12, 6))
    return usual, (chip_rows, chip_rows, min(chip_rows, 2 * cap), cap)


def tied(*groups):
    flat = [v for g in groups for v in g]
    flat = list(lax.optimization_barrier(tuple(flat)))
    out = []
    for g in groups:
        out.append(flat[: len(g)])
        flat = flat[len(g) :]
    return out


def by_ring(tokens, row_adapter_index, base_value_weight, down_factors, up_factors, adapter_scales):
    rows, width = tokens.shape
    own_adapters, rank, _ = down_factors.shape
    cols = base_value_weight.shape[1]
    half, half_cols = width // 2, cols // 2
    peers = lax.axis_size("replica")
    chips = peers // 2
    lines = chips // 2
    hops = chips // 2
    adapters = 2 * own_adapters
    chip_rows = 2 * rows
    cap = 4 * (3 * rows // peers)
    usual, largest = sizes_for(rows, cap)
    me = lax.axis_index("replica")
    core = me % 2
    order = [2 * z for z in range(lines)] + [2 * z + 1 for z in reversed(range(lines))]

    def place(c):
        return jnp.where(c % 2 == 0, c // 2, chips - 1 - c // 2)

    here = place(me // 2)

    def across(v):
        return lax.ppermute(v, "replica", [(i, i ^ 1) for i in range(peers)])

    def around(v, step):
        moves = [
            (2 * order[p] + c, 2 * order[(p + step) % chips] + c)
            for p in range(chips)
            for c in range(2)
        ]
        return lax.ppermute(v, "replica", moves)

    groups = lax.axis_size("groups")
    with jax.named_scope("other_core"):
        other_tokens = across(tokens)
        other_scales = across(adapter_scales)
        up_other = across(up_factors)
        (down_late,), (other_tokens, other_scales, up_other) = tied(
            [down_factors], [other_tokens, other_scales, up_other]
        )
        down_other = across(down_late)

    with jax.named_scope("indices"):
        outgoing = jnp.broadcast_to(row_adapter_index[None, :], (groups * peers, rows))
        every = lax.all_to_all(
            outgoing, ("groups", "replica"), split_axis=0, concat_axis=0, tiled=True
        ).reshape(groups * chips, chip_rows)

    def half_of(v, axis):
        size = v.shape[axis] // 2
        return lax.dynamic_slice_in_dim(v, core * size, size, axis)

    features = jnp.concatenate([half_of(tokens, 1), half_of(other_tokens, 1)], 0)

    kind = jnp.arange(chips)[None, :]
    spot = jnp.arange(chip_rows, dtype=jnp.int32)
    earlier = (spot[None, :] < spot[:, None]).astype(jnp.bfloat16)

    def slots_of(index, position):
        distance = (place(index // adapters) - position) % chips
        marks = distance[:, :, None] == jnp.arange(chips)[None, None, :]
        ahead = jnp.einsum(
            "rs,gsk->grk", earlier, marks.astype(jnp.bfloat16), preferred_element_type=jnp.float32
        )
        marks_f = marks.astype(jnp.float32)
        rank_in = jnp.sum(ahead * marks_f, axis=2)
        count = jnp.sum(marks_f, axis=1)

        def over(mask):
            return jnp.sum(count * mask, axis=1, keepdims=True)

        right = [over((kind >= h) & (kind < hops)) for h in range(1, hops)]
        left = [over((kind > hops) & (kind <= chips - h)) for h in range(1, hops)]
        at_far = count[:, hops : hops + 1]
        right_room = jnp.full_like(at_far, usual[-1])
        left_room = right_room
        for h in range(1, hops):
            right_room = jnp.minimum(right_room, usual[h - 1] - right[h - 1])
            left_room = jnp.minimum(left_room, usual[h - 1] - left[h - 1])
        split = jnp.floor((sum(left) - sum(right) + hops * at_far) / (2.0 * hops))
        split = jnp.minimum(jnp.maximum(split, at_far - left_room), right_room)
        split = jnp.clip(split, 0.0, at_far)
        most = [jnp.maximum(r + split, l + at_far - split) for r, l in zip(right, left)]
        most = jnp.concatenate(most + [jnp.maximum(split, at_far - split)], 1)
        slot = rank_in + jnp.where(
            distance == 0,
            2.0 * chip_rows,
            jnp.where((distance == hops) & (rank_in >= split), chip_rows - split, 0.0),
        )
        for h in range(1, hops):
            beyond = right[h] if h + 1 < hops else 0.0
            slot = slot + jnp.where(distance == h, beyond + split, 0.0)
            beyond = left[h] if h + 1 < hops else 0.0
            slot = slot + jnp.where(distance == chips - h, beyond + at_far - split + chip_rows, 0.0)
        return slot.astype(jnp.int32), distance, most

    with jax.named_scope("all_slots"):
        positions = place(jnp.arange(groups * chips, dtype=jnp.int32) % chips)[:, None]
        all_slots, all_distances, most = slots_of(every, positions)
        overfull = jnp.any(most > jnp.asarray([usual], jnp.float32))

        def from_here(table):
            table = lax.dynamic_slice_in_dim(table, lax.axis_index("groups") * chips, chips, 0)
            ring = [table[c : c + 1] for c in order]
            return lax.dynamic_slice_in_dim(jnp.concatenate(ring + ring, 0), here, chips, 0)

        slots_here = from_here(all_slots)
        slot = jnp.where(core == 0, slots_here[0], jnp.roll(slots_here[0], rows))
        toward = (chips - jnp.arange(chips, dtype=jnp.int32))[:, None] % chips
        items_here = jnp.where(
            from_here(all_distances) == toward, from_here(every % adapters) + 1, 0
        )

    ways = (1, -1)

    def labels(tables, side, line, first, size):
        slots_here, items_here = tables
        at = side + first + jnp.arange(size, dtype=jnp.int32)
        hit = at[:, None] == slots_here[line][None, :]
        return jnp.sum(jnp.where(hit, items_here[line][None, :], 0), axis=1) - 1

    def chosen_by(label):
        turned = jnp.where(core == 0, label, (label + own_adapters) % adapters)
        return (label >= 0)[:, None] & (turned[:, None] == jnp.arange(adapters)[None, :])

    def packed(features, slot, base, first, size):
        hit = (base + first + jnp.arange(size, dtype=jnp.int32))[:, None] == slot[None, :]
        return jnp.dot(
            hit.astype(jnp.bfloat16), features, preferred_element_type=jnp.float32
        ).astype(jnp.bfloat16)

    def low_part(x, label, down):
        chosen = chosen_by(label)
        wide = lax.dot_general(
            x, down, (((1,), (1,)), ((), ())), preferred_element_type=jnp.float32
        )
        return jnp.sum(
            wide.reshape(x.shape[0], adapters, rank) * chosen.astype(jnp.float32)[:, :, None],
            axis=1,
        )

    def exchange(tier, features, slot, slots_here, items_here, tokens, weight, down_own, down_other, up_own, up_other, scales):
        most_rows, second, third, far = tier

        def part(slot, first, last):
            return [
                packed(features, slot, 0 if d > 0 else chip_rows, first, last - first)
                for d in ways
            ]

        def onward(blocks, step=1):
            return [around(v, step * d) for v, d in zip(blocks, ways)]

        def label_of(h, first, size):
            return jnp.concatenate(
                [
                    labels(tables, 0, chips - h, first, size),
                    labels(tables, chip_rows, h, first, size),
                ],
                0,
            )

        def low_of(h, first, blocks, down):
            label = label_of(h, first, blocks[0].shape[0])
            return low_part(jnp.concatenate(blocks, 0), label, down)

        def delta_of(low, label):
            chosen = chosen_by(label)
            total = low + across(low)
            factor = jnp.sum(jnp.where(chosen, scales[None, :], 0.0), axis=1)
            scaled = (total * factor[:, None]).astype(jnp.bfloat16)
            spread = (scaled[:, None, :] * chosen.astype(jnp.bfloat16)[:, :, None]).reshape(
                -1, adapters * rank
            )
            return jnp.dot(spread, up, preferred_element_type=jnp.float32).astype(jnp.bfloat16)

        def both_ways(low, h, first):
            size = low.shape[0] // 2
            delta = delta_of(low, label_of(h, first, size))
            return [delta[:size], delta[size:]]

        def added(small, large):
            return [
                b + jnp.pad(a, ((0, b.shape[0] - a.shape[0]), (0, 0)))
                for a, b in zip(small, large)
            ]

        sent = part(slot, 0, third)
        (down_own, up_own, slot_late), sent = tied([down_own, up_own, slot], sent)
        first_hop = onward(sent)
        down = jnp.concatenate([half_of(down_own, 2), half_of(down_other, 2)], 0)
        down = down.reshape(adapters * rank, half)
        up = jnp.concatenate([half_of(up_own, 2), half_of(up_other, 2)], 0)
        up = up.reshape(adapters * rank, half_cols)
        near = part(slot_late, third, most_rows)
        own_rows = packed(features, slot_late, 2 * chip_rows, 0, cap)
        tables, (own_rows,) = tied([slots_here, items_here], [own_rows])
        own_label = labels(tables, 2 * chip_rows, 0, 0, cap)
        (tokens, down, up, own_rows, *near), first_hop = tied(
            [tokens, down, up, own_rows, *near], first_hop
        )
        second_hop = onward(first_hop)
        near_hop = onward(near)
        low_1 = low_of(1, 0, first_hop, down)
        own_low = low_part(own_rows, own_label, down)
        base = jnp.dot(tokens, weight, preferred_element_type=jnp.float32)
        (low_1, own_low, base), second_hop = tied([low_1, own_low, base], second_hop)
        third_hop = onward(second_hop)
        low_2 = low_of(2, 0, second_hop, down)
        (low_2,), near_hop = tied([low_2], near_hop)
        farther, near_hop = tied([v[: second - third] for v in near_hop], near_hop)
        near_second = onward(farther)
        low_near = low_of(1, third, near_hop, down)
        (low_near,), third_hop = tied([low_near], third_hop)
        farthest, third_hop = tied([v[:far] for v in third_hop], third_hop)
        fourth_hop = onward(farthest)
        low_3 = low_of(3, 0, third_hop, down)
        (low_3,), near_second = tied([low_3], near_second)
        back_3 = onward(both_ways(low_3, 3, 0), -3)
        low_near_2 = low_of(2, third, near_second, down)
        (low_near_2,), fourth_hop = tied([low_near_2], fourth_hop)
        delta_near_2 = both_ways(low_near_2, 2, third)
        back_2 = onward(
            [jnp.concatenate(v, 0) for v in zip(both_ways(low_2, 2, 0), delta_near_2)], -1
        )
        delta_4 = both_ways(low_of(4, 0, fourth_hop, down), 4, 0)
        back_4 = onward(delta_4, -4)
        _, back_2, back_3 = tied(delta_4, back_2, back_3)
        back = [jnp.concatenate(v, 0) for v in zip(both_ways(low_1, 1, 0), both_ways(low_near, 1, third))]
        back = onward(added(back_2, back), -1)
        back = added(back_4, added(back_3, back))
        own_delta = delta_of(own_low, own_label)
        finished = jnp.concatenate([*back, own_delta], 0)
        column = jnp.where(
            slot < chip_rows,
            slot,
            jnp.where(
                slot < 2 * chip_rows,
                slot - chip_rows + most_rows,
                slot - 2 * chip_rows + 2 * most_rows,
            ),
        )
        hit = (column[:, None] == jnp.arange(finished.shape[0], dtype=jnp.int32)[None, :]).astype(
            jnp.bfloat16
        )

        def taken(h):
            return jnp.dot(h, finished, preferred_element_type=jnp.float32).astype(jnp.bfloat16)

        given = across(taken(hit[rows:]))
        kept = taken(hit[:rows])
        delta = jnp.where(
            core == 0,
            jnp.concatenate([kept, given], 1),
            jnp.concatenate([given, kept], 1),
        )
        return (base + delta.astype(jnp.float32)).astype(jnp.bfloat16)

    given = (
        lax.optimization_barrier(features),
        slot,
        slots_here,
        items_here,
        tokens,
        base_value_weight,
        down_factors,
        down_other,
        up_factors,
        up_other,
        jnp.concatenate([adapter_scales, other_scales], 0),
    )
    values = exchange(usual, *given)
    return lax.cond(
        overfull,
        lambda kept, *rest: exchange(largest, *rest),
        lambda kept, *rest: kept,
        values,
        *given,
    )


def by_all_to_all(
    tokens, row_adapter_index, base_value_weight, down_factors, up_factors, adapter_scales
):
    peers = lax.axis_size("replica")
    input_rows = tokens.shape[0]
    feature_width = tokens.shape[1]
    rows_per_replica = down_factors.shape[0]
    rank_index = down_factors.shape[1]
    capacity = 3 * input_rows // peers
    slots = peers * capacity
    holder = row_adapter_index // rows_per_replica
    local_slot = row_adapter_index % rows_per_replica
    dest_table = (holder[:, None] == jnp.arange(peers, dtype=jnp.int32)[None, :]).astype(jnp.int32)
    position = jnp.sum(jnp.cumsum(dest_table, axis=0) * dest_table, axis=1) - 1
    target = holder * capacity + position
    outbox = jnp.zeros((slots, feature_width), tokens.dtype).at[target].set(tokens)
    labels = jnp.full((slots,), -1, jnp.int32).at[target].set(local_slot)
    inbox, in_labels = (
        lax.all_to_all(
            outbox.reshape(peers, capacity, feature_width),
            "replica",
            split_axis=0,
            concat_axis=0,
            tiled=True,
        ),
        lax.all_to_all(
            labels.reshape(peers, capacity), "replica", split_axis=0, concat_axis=0, tiled=True
        ),
    )
    received = inbox.reshape(slots, feature_width)
    marks = in_labels.reshape(slots)
    selected_adapters = (
        marks[:, None] == jnp.arange(rows_per_replica, dtype=jnp.int32)[None, :]
    ).astype(jnp.float32)
    stacked_down_factors = down_factors.reshape(rows_per_replica * rank_index, feature_width)
    wide = lax.dot_general(
        received, stacked_down_factors, (((1,), (1,)), ((), ())), preferred_element_type=jnp.float32
    )
    partial_low = jnp.sum(
        wide.reshape(slots, rows_per_replica, rank_index) * selected_adapters[:, :, None], axis=1
    )
    low_rank_output = lax.psum(partial_low, "tensor")
    scale_factor = jnp.sum(selected_adapters * adapter_scales[None, :], axis=1)
    scaled_output = (low_rank_output * scale_factor[:, None]).astype(jnp.bfloat16)
    spread_rows = (
        scaled_output[:, None, :] * selected_adapters[:, :, None].astype(jnp.bfloat16)
    ).reshape(slots, rows_per_replica * rank_index)
    delta = jnp.dot(
        spread_rows,
        up_factors.reshape(rows_per_replica * rank_index, up_factors.shape[2]),
        preferred_element_type=jnp.float32,
    )
    base_part = jnp.dot(received, base_value_weight, preferred_element_type=jnp.float32)
    base_cols = lax.psum_scatter(base_part, "tensor", scatter_dimension=1, tiled=True)
    finished = base_cols + delta
    returned = lax.all_to_all(
        finished.reshape(peers, capacity, finished.shape[1]).astype(jnp.bfloat16),
        "replica",
        split_axis=0,
        concat_axis=0,
        tiled=True,
    ).astype(jnp.float32)
    total = returned.reshape(slots, finished.shape[1])[target]
    return total.astype(jnp.bfloat16)


def solution(mesh):
    in_specs = (
        P(("groups", "replica"), "tensor"),
        P(("groups", "replica")),
        P("tensor", None),
        P("replica", None, "tensor"),
        P("replica", None, "tensor"),
        P("replica"),
    )
    out_specs = P(("groups", "replica"), "tensor")
    whole_rows = mesh.shape["tensor"] == 1 and mesh.shape["replica"] == 16
    return jax.shard_map(
        by_ring if whole_rows else by_all_to_all,
        mesh=mesh,
        in_specs=in_specs,
        out_specs=out_specs,
        check_vma=False,
    )
```

```python
import jax
import jax.numpy as jnp
from jax import lax
from jax.sharding import PartitionSpec as P


def sizes_for(rows, cap):
    chip_rows = 2 * rows
    unit = chip_rows // 32
    usual = tuple(unit * s for s in (23, 18, 12, 6))
    return usual, (chip_rows, chip_rows, min(chip_rows, 2 * cap), cap)


def tied(*groups):
    flat = [v for g in groups for v in g]
    flat = list(lax.optimization_barrier(tuple(flat)))
    out = []
    for g in groups:
        out.append(flat[: len(g)])
        flat = flat[len(g) :]
    return out


def by_ring(tokens, row_adapter_index, base_value_weight, down_factors, up_factors, adapter_scales):
    rows, width = tokens.shape
    own_adapters, rank, _ = down_factors.shape
    cols = base_value_weight.shape[1]
    half, half_cols = width // 2, cols // 2
    peers = lax.axis_size("replica")
    chips = peers // 2
    lines = chips // 2
    hops = chips // 2
    adapters = 2 * own_adapters
    chip_rows = 2 * rows
    cap = 4 * (3 * rows // peers)
    usual, largest = sizes_for(rows, cap)
    me = lax.axis_index("replica")
    core = me % 2
    order = [2 * z for z in range(lines)] + [2 * z + 1 for z in reversed(range(lines))]

    def place(c):
        return jnp.where(c % 2 == 0, c // 2, chips - 1 - c // 2)

    here = place(me // 2)

    def across(v):
        return lax.ppermute(v, "replica", [(i, i ^ 1) for i in range(peers)])

    def around(v, step):
        moves = [
            (2 * order[p] + c, 2 * order[(p + step) % chips] + c)
            for p in range(chips)
            for c in range(2)
        ]
        return lax.ppermute(v, "replica", moves)

    groups = lax.axis_size("groups")
    with jax.named_scope("other_core"):
        other_tokens = across(tokens)
        other_scales = across(adapter_scales)
        up_other = across(up_factors)
        (down_late,), (other_tokens, other_scales, up_other) = tied(
            [down_factors], [other_tokens, other_scales, up_other]
        )
        down_other = across(down_late)

    with jax.named_scope("indices"):
        outgoing = jnp.broadcast_to(row_adapter_index[None, :], (groups * peers, rows))
        every = lax.all_to_all(
            outgoing, ("groups", "replica"), split_axis=0, concat_axis=0, tiled=True
        ).reshape(groups * chips, chip_rows)

    def half_of(v, axis):
        size = v.shape[axis] // 2
        return lax.dynamic_slice_in_dim(v, core * size, size, axis)

    features = jnp.concatenate([half_of(tokens, 1), half_of(other_tokens, 1)], 0)

    kind = jnp.arange(chips)[None, :]
    spot = jnp.arange(chip_rows, dtype=jnp.int32)
    earlier = (spot[None, :] < spot[:, None]).astype(jnp.bfloat16)

    def slots_of(index, position):
        distance = (place(index // adapters) - position) % chips
        marks = distance[:, :, None] == jnp.arange(chips)[None, None, :]
        ahead = jnp.einsum(
            "rs,gsk->grk", earlier, marks.astype(jnp.bfloat16), preferred_element_type=jnp.float32
        )
        marks_f = marks.astype(jnp.float32)
        rank_in = jnp.sum(ahead * marks_f, axis=2)
        count = jnp.sum(marks_f, axis=1)

        def over(mask):
            return jnp.sum(count * mask, axis=1, keepdims=True)

        right = [over((kind >= h) & (kind < hops)) for h in range(1, hops)]
        left = [over((kind > hops) & (kind <= chips - h)) for h in range(1, hops)]
        at_far = count[:, hops : hops + 1]
        right_room = jnp.full_like(at_far, usual[-1])
        left_room = right_room
        for h in range(1, hops):
            right_room = jnp.minimum(right_room, usual[h - 1] - right[h - 1])
            left_room = jnp.minimum(left_room, usual[h - 1] - left[h - 1])
        split = jnp.floor((sum(left) - sum(right) + hops * at_far) / (2.0 * hops))
        split = jnp.minimum(jnp.maximum(split, at_far - left_room), right_room)
        split = jnp.clip(split, 0.0, at_far)
        most = [jnp.maximum(r + split, l + at_far - split) for r, l in zip(right, left)]
        most = jnp.concatenate(most + [jnp.maximum(split, at_far - split)], 1)
        slot = rank_in + jnp.where(
            distance == 0,
            2.0 * chip_rows,
            jnp.where((distance == hops) & (rank_in >= split), chip_rows - split, 0.0),
        )
        for h in range(1, hops):
            beyond = right[h] if h + 1 < hops else 0.0
            slot = slot + jnp.where(distance == h, beyond + split, 0.0)
            beyond = left[h] if h + 1 < hops else 0.0
            slot = slot + jnp.where(distance == chips - h, beyond + at_far - split + chip_rows, 0.0)
        return slot.astype(jnp.int32), distance, most

    with jax.named_scope("all_slots"):
        positions = place(jnp.arange(groups * chips, dtype=jnp.int32) % chips)[:, None]
        all_slots, all_distances, most = slots_of(every, positions)
        overfull = jnp.any(most > jnp.asarray([usual], jnp.float32))

        def from_here(table):
            table = lax.dynamic_slice_in_dim(table, lax.axis_index("groups") * chips, chips, 0)
            ring = [table[c : c + 1] for c in order]
            return lax.dynamic_slice_in_dim(jnp.concatenate(ring + ring, 0), here, chips, 0)

        slots_here = from_here(all_slots)
        slot = jnp.where(core == 0, slots_here[0], jnp.roll(slots_here[0], rows))
        toward = (chips - jnp.arange(chips, dtype=jnp.int32))[:, None] % chips
        items_here = jnp.where(
            from_here(all_distances) == toward, from_here(every % adapters) + 1, 0
        )

    ways = (1, -1)

    def labels(tables, side, line, first, size):
        slots_here, items_here = tables
        at = side + first + jnp.arange(size, dtype=jnp.int32)
        hit = at[:, None] == slots_here[line][None, :]
        return jnp.sum(jnp.where(hit, items_here[line][None, :], 0), axis=1) - 1

    def chosen_by(label):
        turned = jnp.where(core == 0, label, (label + own_adapters) % adapters)
        return (label >= 0)[:, None] & (turned[:, None] == jnp.arange(adapters)[None, :])

    def packed(features, slot, base, first, size):
        hit = (base + first + jnp.arange(size, dtype=jnp.int32))[:, None] == slot[None, :]
        return jnp.dot(
            hit.astype(jnp.bfloat16), features, preferred_element_type=jnp.float32
        ).astype(jnp.bfloat16)

    def low_part(x, label, down):
        chosen = chosen_by(label)
        wide = lax.dot_general(
            x, down, (((1,), (1,)), ((), ())), preferred_element_type=jnp.float32
        )
        return jnp.sum(
            wide.reshape(x.shape[0], adapters, rank) * chosen.astype(jnp.float32)[:, :, None],
            axis=1,
        )

    def exchange(tier, features, slot, slots_here, items_here, tokens, weight, down_own, down_other, up_own, up_other, scales):
        most_rows, second, third, far = tier

        def part(slot, first, last):
            return [
                packed(features, slot, 0 if d > 0 else chip_rows, first, last - first)
                for d in ways
            ]

        def onward(blocks, step=1):
            return [around(v, step * d) for v, d in zip(blocks, ways)]

        def label_of(h, first, size):
            return jnp.concatenate(
                [
                    labels(tables, 0, chips - h, first, size),
                    labels(tables, chip_rows, h, first, size),
                ],
                0,
            )

        def low_of(h, first, blocks, down):
            label = label_of(h, first, blocks[0].shape[0])
            return low_part(jnp.concatenate(blocks, 0), label, down)

        def delta_of(low, label):
            chosen = chosen_by(label)
            total = low + across(low)
            factor = jnp.sum(jnp.where(chosen, scales[None, :], 0.0), axis=1)
            scaled = (total * factor[:, None]).astype(jnp.bfloat16)
            spread = (scaled[:, None, :] * chosen.astype(jnp.bfloat16)[:, :, None]).reshape(
                -1, adapters * rank
            )
            return jnp.dot(spread, up, preferred_element_type=jnp.float32).astype(jnp.bfloat16)

        def both_ways(low, h, first):
            size = low.shape[0] // 2
            delta = delta_of(low, label_of(h, first, size))
            return [delta[:size], delta[size:]]

        def added(small, large):
            return [
                b + jnp.pad(a, ((0, b.shape[0] - a.shape[0]), (0, 0)))
                for a, b in zip(small, large)
            ]

        sent = part(slot, 0, third)
        (down_own, up_own, slot_late), sent = tied([down_own, up_own, slot], sent)
        first_hop = onward(sent)
        down = jnp.concatenate([half_of(down_own, 2), half_of(down_other, 2)], 0)
        down = down.reshape(adapters * rank, half)
        up = jnp.concatenate([half_of(up_own, 2), half_of(up_other, 2)], 0)
        up = up.reshape(adapters * rank, half_cols)
        near = part(slot_late, third, most_rows)
        own_rows = packed(features, slot_late, 2 * chip_rows, 0, cap)
        tables, (own_rows,) = tied([slots_here, items_here], [own_rows])
        own_label = labels(tables, 2 * chip_rows, 0, 0, cap)
        (tokens, down, up, own_rows, *near), first_hop = tied(
            [tokens, down, up, own_rows, *near], first_hop
        )
        second_hop = onward(first_hop)
        near_hop = onward(near)
        low_1 = low_of(1, 0, first_hop, down)
        own_low = low_part(own_rows, own_label, down)
        base = jnp.dot(tokens, weight, preferred_element_type=jnp.float32)
        (low_1, own_low, base), second_hop = tied([low_1, own_low, base], second_hop)
        third_hop = onward(second_hop)
        low_2 = low_of(2, 0, second_hop, down)
        (low_2,), near_hop = tied([low_2], near_hop)
        farther, near_hop = tied([v[: second - third] for v in near_hop], near_hop)
        near_second = onward(farther)
        low_near = low_of(1, third, near_hop, down)
        (low_near,), third_hop = tied([low_near], third_hop)
        farthest, third_hop = tied([v[:far] for v in third_hop], third_hop)
        fourth_hop = onward(farthest)
        low_3 = low_of(3, 0, third_hop, down)
        (low_3,), near_second = tied([low_3], near_second)
        back_3 = onward(both_ways(low_3, 3, 0), -1)
        low_near_2 = low_of(2, third, near_second, down)
        (low_near_2,), fourth_hop = tied([low_near_2], fourth_hop)
        delta_2 = [
            jnp.concatenate(v, 0)
            for v in zip(both_ways(low_2, 2, 0), both_ways(low_near_2, 2, third))
        ]
        delta_1 = [
            jnp.concatenate(v, 0)
            for v in zip(both_ways(low_1, 1, 0), both_ways(low_near, 1, third))
        ]
        low_4 = low_of(4, 0, fourth_hop, down)
        back_2 = onward(added(back_3, delta_2), -1)
        delta_4 = both_ways(low_4, 4, 0)
        back_4 = onward(delta_4, -4)
        (back_4, back_2, delta_1) = tied(back_4, back_2, delta_1)
        back = added(back_4, onward(added(back_2, delta_1), -1))
        own_delta = delta_of(own_low, own_label)
        finished = jnp.concatenate([*back, own_delta], 0)
        column = jnp.where(
            slot < chip_rows,
            slot,
            jnp.where(
                slot < 2 * chip_rows,
                slot - chip_rows + most_rows,
                slot - 2 * chip_rows + 2 * most_rows,
            ),
        )
        hit = (column[:, None] == jnp.arange(finished.shape[0], dtype=jnp.int32)[None, :]).astype(
            jnp.bfloat16
        )

        def taken(h):
            return jnp.dot(h, finished, preferred_element_type=jnp.float32).astype(jnp.bfloat16)

        given = across(taken(hit[rows:]))
        kept = taken(hit[:rows])
        delta = jnp.where(
            core == 0,
            jnp.concatenate([kept, given], 1),
            jnp.concatenate([given, kept], 1),
        )
        return (base + delta.astype(jnp.float32)).astype(jnp.bfloat16)

    given = (
        lax.optimization_barrier(features),
        slot,
        slots_here,
        items_here,
        tokens,
        base_value_weight,
        down_factors,
        down_other,
        up_factors,
        up_other,
        jnp.concatenate([adapter_scales, other_scales], 0),
    )
    values = exchange(usual, *given)
    return lax.cond(
        overfull,
        lambda kept, *rest: exchange(largest, *rest),
        lambda kept, *rest: kept,
        values,
        *given,
    )


def by_all_to_all(
    tokens, row_adapter_index, base_value_weight, down_factors, up_factors, adapter_scales
):
    peers = lax.axis_size("replica")
    input_rows = tokens.shape[0]
    feature_width = tokens.shape[1]
    rows_per_replica = down_factors.shape[0]
    rank_index = down_factors.shape[1]
    capacity = 3 * input_rows // peers
    slots = peers * capacity
    holder = row_adapter_index // rows_per_replica
    local_slot = row_adapter_index % rows_per_replica
    dest_table = (holder[:, None] == jnp.arange(peers, dtype=jnp.int32)[None, :]).astype(jnp.int32)
    position = jnp.sum(jnp.cumsum(dest_table, axis=0) * dest_table, axis=1) - 1
    target = holder * capacity + position
    outbox = jnp.zeros((slots, feature_width), tokens.dtype).at[target].set(tokens)
    labels = jnp.full((slots,), -1, jnp.int32).at[target].set(local_slot)
    inbox, in_labels = (
        lax.all_to_all(
            outbox.reshape(peers, capacity, feature_width),
            "replica",
            split_axis=0,
            concat_axis=0,
            tiled=True,
        ),
        lax.all_to_all(
            labels.reshape(peers, capacity), "replica", split_axis=0, concat_axis=0, tiled=True
        ),
    )
    received = inbox.reshape(slots, feature_width)
    marks = in_labels.reshape(slots)
    selected_adapters = (
        marks[:, None] == jnp.arange(rows_per_replica, dtype=jnp.int32)[None, :]
    ).astype(jnp.float32)
    stacked_down_factors = down_factors.reshape(rows_per_replica * rank_index, feature_width)
    wide = lax.dot_general(
        received, stacked_down_factors, (((1,), (1,)), ((), ())), preferred_element_type=jnp.float32
    )
    partial_low = jnp.sum(
        wide.reshape(slots, rows_per_replica, rank_index) * selected_adapters[:, :, None], axis=1
    )
    low_rank_output = lax.psum(partial_low, "tensor")
    scale_factor = jnp.sum(selected_adapters * adapter_scales[None, :], axis=1)
    scaled_output = (low_rank_output * scale_factor[:, None]).astype(jnp.bfloat16)
    spread_rows = (
        scaled_output[:, None, :] * selected_adapters[:, :, None].astype(jnp.bfloat16)
    ).reshape(slots, rows_per_replica * rank_index)
    delta = jnp.dot(
        spread_rows,
        up_factors.reshape(rows_per_replica * rank_index, up_factors.shape[2]),
        preferred_element_type=jnp.float32,
    )
    base_part = jnp.dot(received, base_value_weight, preferred_element_type=jnp.float32)
    base_cols = lax.psum_scatter(base_part, "tensor", scatter_dimension=1, tiled=True)
    finished = base_cols + delta
    returned = lax.all_to_all(
        finished.reshape(peers, capacity, finished.shape[1]).astype(jnp.bfloat16),
        "replica",
        split_axis=0,
        concat_axis=0,
        tiled=True,
    ).astype(jnp.float32)
    total = returned.reshape(slots, finished.shape[1])[target]
    return total.astype(jnp.bfloat16)


def solution(mesh):
    in_specs = (
        P(("groups", "replica"), "tensor"),
        P(("groups", "replica")),
        P("tensor", None),
        P("replica", None, "tensor"),
        P("replica", None, "tensor"),
        P("replica"),
    )
    out_specs = P(("groups", "replica"), "tensor")
    whole_rows = mesh.shape["tensor"] == 1 and mesh.shape["replica"] == 16
    return jax.shard_map(
        by_ring if whole_rows else by_all_to_all,
        mesh=mesh,
        in_specs=in_specs,
        out_specs=out_specs,
        check_vma=False,
    )
```

```python
import jax
import jax.numpy as jnp
from jax import lax
from jax.sharding import PartitionSpec as P


def sizes_for(rows, cap):
    chip_rows = 2 * rows
    unit = chip_rows // 32
    usual = tuple(unit * s for s in (23, 18, 12, 6))
    return usual, (chip_rows, chip_rows, min(chip_rows, 2 * cap), cap)


def tied(*groups):
    flat = [v for g in groups for v in g]
    flat = list(lax.optimization_barrier(tuple(flat)))
    out = []
    for g in groups:
        out.append(flat[: len(g)])
        flat = flat[len(g) :]
    return out


def by_ring(tokens, row_adapter_index, base_value_weight, down_factors, up_factors, adapter_scales):
    rows, width = tokens.shape
    own_adapters, rank, _ = down_factors.shape
    cols = base_value_weight.shape[1]
    half, half_cols = width // 2, cols // 2
    peers = lax.axis_size("replica")
    chips = peers // 2
    lines = chips // 2
    hops = chips // 2
    adapters = 2 * own_adapters
    chip_rows = 2 * rows
    cap = 4 * (3 * rows // peers)
    usual, largest = sizes_for(rows, cap)
    me = lax.axis_index("replica")
    core = me % 2
    order = [2 * z for z in range(lines)] + [2 * z + 1 for z in reversed(range(lines))]

    def place(c):
        return jnp.where(c % 2 == 0, c // 2, chips - 1 - c // 2)

    here = place(me // 2)

    def across(v):
        return lax.ppermute(v, "replica", [(i, i ^ 1) for i in range(peers)])

    def around(v, step):
        moves = [
            (2 * order[p] + c, 2 * order[(p + step) % chips] + c)
            for p in range(chips)
            for c in range(2)
        ]
        return lax.ppermute(v, "replica", moves)

    groups = lax.axis_size("groups")
    with jax.named_scope("other_core"):
        other_index = across(row_adapter_index)
        other_tokens = across(tokens)
        other_scales = across(adapter_scales)
        up_other = across(up_factors)
        (down_late,), (other_tokens, other_scales, up_other) = tied(
            [down_factors], [other_tokens, other_scales, up_other]
        )
        down_other = across(down_late)

    with jax.named_scope("indices"):
        outgoing = jnp.broadcast_to(row_adapter_index[None, :], (groups * peers, rows))
        every = lax.all_to_all(
            outgoing, ("groups", "replica"), split_axis=0, concat_axis=0, tiled=True
        ).reshape(groups * chips, chip_rows)

    def half_of(v, axis):
        size = v.shape[axis] // 2
        return lax.dynamic_slice_in_dim(v, core * size, size, axis)

    features = jnp.concatenate([half_of(tokens, 1), half_of(other_tokens, 1)], 0)

    kind = jnp.arange(chips)[None, :]
    spot = jnp.arange(chip_rows, dtype=jnp.int32)
    earlier = (spot[None, :] < spot[:, None]).astype(jnp.bfloat16)

    def slots_of(index, position):
        distance = (place(index // adapters) - position) % chips
        marks = distance[:, :, None] == jnp.arange(chips)[None, None, :]
        ahead = jnp.einsum(
            "rs,gsk->grk", earlier, marks.astype(jnp.bfloat16), preferred_element_type=jnp.float32
        )
        marks_f = marks.astype(jnp.float32)
        rank_in = jnp.sum(ahead * marks_f, axis=2)
        count = jnp.sum(marks_f, axis=1)

        def over(mask):
            return jnp.sum(count * mask, axis=1, keepdims=True)

        right = [over((kind >= h) & (kind < hops)) for h in range(1, hops)]
        left = [over((kind > hops) & (kind <= chips - h)) for h in range(1, hops)]
        at_far = count[:, hops : hops + 1]
        right_room = jnp.full_like(at_far, usual[-1])
        left_room = right_room
        for h in range(1, hops):
            right_room = jnp.minimum(right_room, usual[h - 1] - right[h - 1])
            left_room = jnp.minimum(left_room, usual[h - 1] - left[h - 1])
        split = jnp.floor((sum(left) - sum(right) + hops * at_far) / (2.0 * hops))
        split = jnp.minimum(jnp.maximum(split, at_far - left_room), right_room)
        split = jnp.clip(split, 0.0, at_far)
        most = [jnp.maximum(r + split, l + at_far - split) for r, l in zip(right, left)]
        most = jnp.concatenate(most + [jnp.maximum(split, at_far - split)], 1)
        slot = rank_in + jnp.where(
            distance == 0,
            2.0 * chip_rows,
            jnp.where((distance == hops) & (rank_in >= split), chip_rows - split, 0.0),
        )
        for h in range(1, hops):
            beyond = right[h] if h + 1 < hops else 0.0
            slot = slot + jnp.where(distance == h, beyond + split, 0.0)
            beyond = left[h] if h + 1 < hops else 0.0
            slot = slot + jnp.where(distance == chips - h, beyond + at_far - split + chip_rows, 0.0)
        return slot.astype(jnp.int32), distance, most

    with jax.named_scope("own_slots"):
        both = jnp.where(
            core == 0,
            jnp.concatenate([row_adapter_index, other_index], 0),
            jnp.concatenate([other_index, row_adapter_index], 0),
        )
        lines_here = jnp.stack([here, (here + 1) % chips])[:, None]
        slot = slots_of(jnp.stack([both, both]), lines_here)[0][0]
        slot = jnp.where(core == 0, slot, jnp.roll(slot, rows))

    def tables_of(every):
        positions = place(jnp.arange(groups * chips, dtype=jnp.int32) % chips)[:, None]
        all_slots, all_distances, most = slots_of(every, positions)
        overfull = jnp.any(most > jnp.asarray([usual], jnp.float32))

        def from_here(table):
            table = lax.dynamic_slice_in_dim(table, lax.axis_index("groups") * chips, chips, 0)
            ring = [table[c : c + 1] for c in order]
            return lax.dynamic_slice_in_dim(jnp.concatenate(ring + ring, 0), here, chips, 0)

        toward = (chips - jnp.arange(chips, dtype=jnp.int32))[:, None] % chips
        items_here = jnp.where(
            from_here(all_distances) == toward, from_here(every % adapters) + 1, 0
        )
        return from_here(all_slots), items_here, overfull

    ways = (1, -1)

    def labels(tables, side, line, first, size):
        slots_here, items_here = tables
        at = side + first + jnp.arange(size, dtype=jnp.int32)
        hit = at[:, None] == slots_here[line][None, :]
        return jnp.sum(jnp.where(hit, items_here[line][None, :], 0), axis=1) - 1

    def chosen_by(label):
        turned = jnp.where(core == 0, label, (label + own_adapters) % adapters)
        return (label >= 0)[:, None] & (turned[:, None] == jnp.arange(adapters)[None, :])

    def packed(features, slot, base, first, size):
        hit = (base + first + jnp.arange(size, dtype=jnp.int32))[:, None] == slot[None, :]
        return jnp.dot(
            hit.astype(jnp.bfloat16), features, preferred_element_type=jnp.float32
        ).astype(jnp.bfloat16)

    def low_part(x, label, down):
        chosen = chosen_by(label)
        wide = lax.dot_general(
            x, down, (((1,), (1,)), ((), ())), preferred_element_type=jnp.float32
        )
        return jnp.sum(
            wide.reshape(x.shape[0], adapters, rank) * chosen.astype(jnp.float32)[:, :, None],
            axis=1,
        )

    def exchange(tier, features, slot, every, tokens, weight, down_own, down_other, up_own, up_other, scales):
        most_rows, second, third, far = tier

        def part(slot, first, last):
            return [
                packed(features, slot, 0 if d > 0 else chip_rows, first, last - first)
                for d in ways
            ]

        def onward(blocks, step=1):
            return [around(v, step * d) for v, d in zip(blocks, ways)]

        def label_of(h, first, size):
            return jnp.concatenate(
                [
                    labels(tables, 0, chips - h, first, size),
                    labels(tables, chip_rows, h, first, size),
                ],
                0,
            )

        def low_of(h, first, blocks, down):
            label = label_of(h, first, blocks[0].shape[0])
            return low_part(jnp.concatenate(blocks, 0), label, down)

        def delta_of(low, label):
            chosen = chosen_by(label)
            total = low + across(low)
            factor = jnp.sum(jnp.where(chosen, scales[None, :], 0.0), axis=1)
            scaled = (total * factor[:, None]).astype(jnp.bfloat16)
            spread = (scaled[:, None, :] * chosen.astype(jnp.bfloat16)[:, :, None]).reshape(
                -1, adapters * rank
            )
            return jnp.dot(spread, up, preferred_element_type=jnp.float32).astype(jnp.bfloat16)

        def both_ways(low, h, first):
            size = low.shape[0] // 2
            delta = delta_of(low, label_of(h, first, size))
            return [delta[:size], delta[size:]]

        def added(small, large):
            return [
                b + jnp.pad(a, ((0, b.shape[0] - a.shape[0]), (0, 0)))
                for a, b in zip(small, large)
            ]

        sent = part(slot, 0, third)
        (down_own, up_own, slot_late, every), sent = tied([down_own, up_own, slot, every], sent)
        first_hop = onward(sent)
        down = jnp.concatenate([half_of(down_own, 2), half_of(down_other, 2)], 0)
        down = down.reshape(adapters * rank, half)
        up = jnp.concatenate([half_of(up_own, 2), half_of(up_other, 2)], 0)
        up = up.reshape(adapters * rank, half_cols)
        near = part(slot_late, third, most_rows)
        own_rows = packed(features, slot_late, 2 * chip_rows, 0, cap)
        (every,), (own_rows,) = tied([every], [own_rows])
        *tables, overfull = tables_of(every)
        own_label = labels(tables, 2 * chip_rows, 0, 0, cap)
        (tokens, down, up, own_rows, *near), first_hop = tied(
            [tokens, down, up, own_rows, *near], first_hop
        )
        second_hop = onward(first_hop)
        near_hop = onward(near)
        low_1 = low_of(1, 0, first_hop, down)
        own_low = low_part(own_rows, own_label, down)
        base = jnp.dot(tokens, weight, preferred_element_type=jnp.float32)
        (low_1, own_low, base), second_hop = tied([low_1, own_low, base], second_hop)
        third_hop = onward(second_hop)
        low_2 = low_of(2, 0, second_hop, down)
        (low_2,), near_hop = tied([low_2], near_hop)
        farther, near_hop = tied([v[: second - third] for v in near_hop], near_hop)
        near_second = onward(farther)
        low_near = low_of(1, third, near_hop, down)
        (low_near,), third_hop = tied([low_near], third_hop)
        farthest, third_hop = tied([v[:far] for v in third_hop], third_hop)
        fourth_hop = onward(farthest)
        low_3 = low_of(3, 0, third_hop, down)
        (low_3,), near_second = tied([low_3], near_second)
        back_3 = onward(both_ways(low_3, 3, 0), -3)
        low_near_2 = low_of(2, third, near_second, down)
        (low_near_2,), fourth_hop = tied([low_near_2], fourth_hop)
        delta_near_2 = both_ways(low_near_2, 2, third)
        back_2 = onward(
            [jnp.concatenate(v, 0) for v in zip(both_ways(low_2, 2, 0), delta_near_2)], -1
        )
        delta_4 = both_ways(low_of(4, 0, fourth_hop, down), 4, 0)
        back_4 = onward(delta_4, -4)
        _, back_2, back_3 = tied(delta_4, back_2, back_3)
        back = [jnp.concatenate(v, 0) for v in zip(both_ways(low_1, 1, 0), both_ways(low_near, 1, third))]
        back = onward(added(back_2, back), -1)
        back = added(back_4, added(back_3, back))
        own_delta = delta_of(own_low, own_label)
        finished = jnp.concatenate([*back, own_delta], 0)
        column = jnp.where(
            slot < chip_rows,
            slot,
            jnp.where(
                slot < 2 * chip_rows,
                slot - chip_rows + most_rows,
                slot - 2 * chip_rows + 2 * most_rows,
            ),
        )
        hit = (column[:, None] == jnp.arange(finished.shape[0], dtype=jnp.int32)[None, :]).astype(
            jnp.bfloat16
        )

        def taken(h):
            return jnp.dot(h, finished, preferred_element_type=jnp.float32).astype(jnp.bfloat16)

        given = across(taken(hit[rows:]))
        kept = taken(hit[:rows])
        delta = jnp.where(
            core == 0,
            jnp.concatenate([kept, given], 1),
            jnp.concatenate([given, kept], 1),
        )
        return (base + delta.astype(jnp.float32)).astype(jnp.bfloat16), overfull

    given = (
        lax.optimization_barrier(features),
        slot,
        every,
        tokens,
        base_value_weight,
        down_factors,
        down_other,
        up_factors,
        up_other,
        jnp.concatenate([adapter_scales, other_scales], 0),
    )
    values, overfull = exchange(usual, *given)
    return lax.cond(
        overfull,
        lambda kept, *rest: exchange(largest, *rest)[0],
        lambda kept, *rest: kept,
        values,
        *given,
    )


def by_all_to_all(
    tokens, row_adapter_index, base_value_weight, down_factors, up_factors, adapter_scales
):
    peers = lax.axis_size("replica")
    input_rows = tokens.shape[0]
    feature_width = tokens.shape[1]
    rows_per_replica = down_factors.shape[0]
    rank_index = down_factors.shape[1]
    capacity = 3 * input_rows // peers
    slots = peers * capacity
    holder = row_adapter_index // rows_per_replica
    local_slot = row_adapter_index % rows_per_replica
    dest_table = (holder[:, None] == jnp.arange(peers, dtype=jnp.int32)[None, :]).astype(jnp.int32)
    position = jnp.sum(jnp.cumsum(dest_table, axis=0) * dest_table, axis=1) - 1
    target = holder * capacity + position
    outbox = jnp.zeros((slots, feature_width), tokens.dtype).at[target].set(tokens)
    labels = jnp.full((slots,), -1, jnp.int32).at[target].set(local_slot)
    inbox, in_labels = (
        lax.all_to_all(
            outbox.reshape(peers, capacity, feature_width),
            "replica",
            split_axis=0,
            concat_axis=0,
            tiled=True,
        ),
        lax.all_to_all(
            labels.reshape(peers, capacity), "replica", split_axis=0, concat_axis=0, tiled=True
        ),
    )
    received = inbox.reshape(slots, feature_width)
    marks = in_labels.reshape(slots)
    selected_adapters = (
        marks[:, None] == jnp.arange(rows_per_replica, dtype=jnp.int32)[None, :]
    ).astype(jnp.float32)
    stacked_down_factors = down_factors.reshape(rows_per_replica * rank_index, feature_width)
    wide = lax.dot_general(
        received, stacked_down_factors, (((1,), (1,)), ((), ())), preferred_element_type=jnp.float32
    )
    partial_low = jnp.sum(
        wide.reshape(slots, rows_per_replica, rank_index) * selected_adapters[:, :, None], axis=1
    )
    low_rank_output = lax.psum(partial_low, "tensor")
    scale_factor = jnp.sum(selected_adapters * adapter_scales[None, :], axis=1)
    scaled_output = (low_rank_output * scale_factor[:, None]).astype(jnp.bfloat16)
    spread_rows = (
        scaled_output[:, None, :] * selected_adapters[:, :, None].astype(jnp.bfloat16)
    ).reshape(slots, rows_per_replica * rank_index)
    delta = jnp.dot(
        spread_rows,
        up_factors.reshape(rows_per_replica * rank_index, up_factors.shape[2]),
        preferred_element_type=jnp.float32,
    )
    base_part = jnp.dot(received, base_value_weight, preferred_element_type=jnp.float32)
    base_cols = lax.psum_scatter(base_part, "tensor", scatter_dimension=1, tiled=True)
    finished = base_cols + delta
    returned = lax.all_to_all(
        finished.reshape(peers, capacity, finished.shape[1]).astype(jnp.bfloat16),
        "replica",
        split_axis=0,
        concat_axis=0,
        tiled=True,
    ).astype(jnp.float32)
    total = returned.reshape(slots, finished.shape[1])[target]
    return total.astype(jnp.bfloat16)


def solution(mesh):
    in_specs = (
        P(("groups", "replica"), "tensor"),
        P(("groups", "replica")),
        P("tensor", None),
        P("replica", None, "tensor"),
        P("replica", None, "tensor"),
        P("replica"),
    )
    out_specs = P(("groups", "replica"), "tensor")
    whole_rows = mesh.shape["tensor"] == 1 and mesh.shape["replica"] == 16
    return jax.shard_map(
        by_ring if whole_rows else by_all_to_all,
        mesh=mesh,
        in_specs=in_specs,
        out_specs=out_specs,
        check_vma=False,
    )
```

```python
import jax
import jax.numpy as jnp
from jax import lax
from jax.sharding import PartitionSpec as P


def sizes_for(rows, cap):
    chip_rows = 2 * rows
    unit = chip_rows // 32
    usual = tuple(unit * s for s in (23, 18, 12, 6))
    return usual, (chip_rows, chip_rows, min(chip_rows, 2 * cap), cap)


def tied(*groups):
    flat = [v for g in groups for v in g]
    flat = list(lax.optimization_barrier(tuple(flat)))
    out = []
    for g in groups:
        out.append(flat[: len(g)])
        flat = flat[len(g) :]
    return out


def by_ring(tokens, row_adapter_index, base_value_weight, down_factors, up_factors, adapter_scales):
    rows, width = tokens.shape
    own_adapters, rank, _ = down_factors.shape
    cols = base_value_weight.shape[1]
    half, half_cols = width // 2, cols // 2
    peers = lax.axis_size("replica")
    chips = peers // 2
    lines = chips // 2
    hops = chips // 2
    adapters = 2 * own_adapters
    chip_rows = 2 * rows
    cap = 4 * (3 * rows // peers)
    usual, largest = sizes_for(rows, cap)
    me = lax.axis_index("replica")
    core = me % 2
    order = [2 * z for z in range(lines)] + [2 * z + 1 for z in reversed(range(lines))]

    def place(c):
        return jnp.where(c % 2 == 0, c // 2, chips - 1 - c // 2)

    here = place(me // 2)

    def across(v):
        return lax.ppermute(v, "replica", [(i, i ^ 1) for i in range(peers)])

    def around(v, step):
        moves = [
            (2 * order[p] + c, 2 * order[(p + step) % chips] + c)
            for p in range(chips)
            for c in range(2)
        ]
        return lax.ppermute(v, "replica", moves)

    groups = lax.axis_size("groups")
    with jax.named_scope("other_core"):
        other_tokens = across(tokens)
        other_scales = across(adapter_scales)
        up_other = across(up_factors)
        (down_late,), (other_tokens, other_scales, up_other) = tied(
            [down_factors], [other_tokens, other_scales, up_other]
        )
        down_other = across(down_late)

    with jax.named_scope("indices"):
        outgoing = jnp.broadcast_to(row_adapter_index[None, :], (groups * peers, rows))
        every = lax.all_to_all(
            outgoing, ("groups", "replica"), split_axis=0, concat_axis=0, tiled=True
        ).reshape(groups * chips, chip_rows)

    def half_of(v, axis):
        size = v.shape[axis] // 2
        return lax.dynamic_slice_in_dim(v, core * size, size, axis)

    features = jnp.concatenate([half_of(tokens, 1), half_of(other_tokens, 1)], 0)

    kind = jnp.arange(chips)[None, :]
    spot = jnp.arange(chip_rows, dtype=jnp.int32)
    earlier = (spot[None, :] < spot[:, None]).astype(jnp.bfloat16)

    def slots_of(index, position):
        distance = (place(index // adapters) - position) % chips
        marks = distance[:, :, None] == jnp.arange(chips)[None, None, :]
        ahead = jnp.einsum(
            "rs,gsk->grk", earlier, marks.astype(jnp.bfloat16), preferred_element_type=jnp.float32
        )
        marks_f = marks.astype(jnp.float32)
        rank_in = jnp.sum(ahead * marks_f, axis=2)
        count = jnp.sum(marks_f, axis=1)

        def over(mask):
            return jnp.sum(count * mask, axis=1, keepdims=True)

        right = [over((kind >= h) & (kind < hops)) for h in range(1, hops)]
        left = [over((kind > hops) & (kind <= chips - h)) for h in range(1, hops)]
        at_far = count[:, hops : hops + 1]
        right_room = jnp.full_like(at_far, usual[-1])
        left_room = right_room
        for h in range(1, hops):
            right_room = jnp.minimum(right_room, usual[h - 1] - right[h - 1])
            left_room = jnp.minimum(left_room, usual[h - 1] - left[h - 1])
        split = jnp.floor((sum(left) - sum(right) + hops * at_far) / (2.0 * hops))
        split = jnp.minimum(jnp.maximum(split, at_far - left_room), right_room)
        split = jnp.clip(split, 0.0, at_far)
        most = [jnp.maximum(r + split, l + at_far - split) for r, l in zip(right, left)]
        most = jnp.concatenate(most + [jnp.maximum(split, at_far - split)], 1)
        slot = rank_in + jnp.where(
            distance == 0,
            2.0 * chip_rows,
            jnp.where((distance == hops) & (rank_in >= split), chip_rows - split, 0.0),
        )
        for h in range(1, hops):
            beyond = right[h] if h + 1 < hops else 0.0
            slot = slot + jnp.where(distance == h, beyond + split, 0.0)
            beyond = left[h] if h + 1 < hops else 0.0
            slot = slot + jnp.where(distance == chips - h, beyond + at_far - split + chip_rows, 0.0)
        return slot.astype(jnp.int32), distance, most

    with jax.named_scope("all_slots"):
        positions = place(jnp.arange(groups * chips, dtype=jnp.int32) % chips)[:, None]
        all_slots, all_distances, most = slots_of(every, positions)
        overfull = jnp.any(most > jnp.asarray([usual], jnp.float32))

        def from_here(table):
            table = lax.dynamic_slice_in_dim(table, lax.axis_index("groups") * chips, chips, 0)
            ring = [table[c : c + 1] for c in order]
            return lax.dynamic_slice_in_dim(jnp.concatenate(ring + ring, 0), here, chips, 0)

        slots_here = from_here(all_slots)
        slot = jnp.where(core == 0, slots_here[0], jnp.roll(slots_here[0], rows))
        toward = (chips - jnp.arange(chips, dtype=jnp.int32))[:, None] % chips
        items_here = jnp.where(
            from_here(all_distances) == toward, from_here(every % adapters) + 1, 0
        )

    ways = (1, -1)

    def labels(tables, side, line, first, size):
        slots_here, items_here = tables
        at = side + first + jnp.arange(size, dtype=jnp.int32)
        hit = at[:, None] == slots_here[line][None, :]
        return jnp.sum(jnp.where(hit, items_here[line][None, :], 0), axis=1) - 1

    def chosen_by(label):
        turned = jnp.where(core == 0, label, (label + own_adapters) % adapters)
        return (label >= 0)[:, None] & (turned[:, None] == jnp.arange(adapters)[None, :])

    def packed(features, slot, base, first, size):
        hit = (base + first + jnp.arange(size, dtype=jnp.int32))[:, None] == slot[None, :]
        return jnp.dot(
            hit.astype(jnp.bfloat16), features, preferred_element_type=jnp.float32
        ).astype(jnp.bfloat16)

    def low_part(x, label, down):
        chosen = chosen_by(label)
        wide = lax.dot_general(
            x, down, (((1,), (1,)), ((), ())), preferred_element_type=jnp.float32
        )
        return jnp.sum(
            wide.reshape(x.shape[0], adapters, rank) * chosen.astype(jnp.float32)[:, :, None],
            axis=1,
        )

    def exchange(tier, features, slot, slots_here, items_here, tokens, weight, down_own, down_other, up_own, up_other, scales):
        most_rows, second, third, far = tier

        def part(slot, first, last):
            return [
                packed(features, slot, 0 if d > 0 else chip_rows, first, last - first)
                for d in ways
            ]

        def onward(blocks, step=1):
            return [around(v, step * d) for v, d in zip(blocks, ways)]

        def label_of(h, first, size):
            return jnp.concatenate(
                [
                    labels(tables, 0, chips - h, first, size),
                    labels(tables, chip_rows, h, first, size),
                ],
                0,
            )

        def low_of(h, first, blocks, down):
            label = label_of(h, first, blocks[0].shape[0])
            return low_part(jnp.concatenate(blocks, 0), label, down)

        def delta_of(low, label):
            chosen = chosen_by(label)
            total = low + across(low)
            factor = jnp.sum(jnp.where(chosen, scales[None, :], 0.0), axis=1)
            scaled = (total * factor[:, None]).astype(jnp.bfloat16)
            spread = (scaled[:, None, :] * chosen.astype(jnp.bfloat16)[:, :, None]).reshape(
                -1, adapters * rank
            )
            return jnp.dot(spread, up, preferred_element_type=jnp.float32).astype(jnp.bfloat16)

        def both_ways(low, h, first):
            size = low.shape[0] // 2
            delta = delta_of(low, label_of(h, first, size))
            return [delta[:size], delta[size:]]

        def added(small, large):
            return [
                b + jnp.pad(a, ((0, b.shape[0] - a.shape[0]), (0, 0)))
                for a, b in zip(small, large)
            ]

        sent = part(slot, 0, third)
        (down_own, up_own, slot_late), sent = tied([down_own, up_own, slot], sent)
        first_hop = onward(sent)
        down = jnp.concatenate([half_of(down_own, 2), half_of(down_other, 2)], 0)
        down = down.reshape(adapters * rank, half)
        near = part(slot_late, third, most_rows)
        own_rows = packed(features, slot_late, 2 * chip_rows, 0, cap)
        tables, (own_rows,) = tied([slots_here, items_here], [own_rows])
        own_label = labels(tables, 2 * chip_rows, 0, 0, cap)
        (tokens, down, own_rows, *near), first_hop = tied(
            [tokens, down, own_rows, *near], first_hop
        )
        second_hop = onward(first_hop)
        near_hop = onward(near)
        low_1 = low_of(1, 0, first_hop, down)
        own_low = low_part(own_rows, own_label, down)
        base = jnp.dot(tokens, weight, preferred_element_type=jnp.float32)
        (low_1, own_low, base, up_own, up_other), second_hop = tied(
            [low_1, own_low, base, up_own, up_other], second_hop
        )
        up = jnp.concatenate([half_of(up_own, 2), half_of(up_other, 2)], 0)
        up = up.reshape(adapters * rank, half_cols)
        third_hop = onward(second_hop)
        low_2 = low_of(2, 0, second_hop, down)
        (low_2, up), near_hop = tied([low_2, up], near_hop)
        farther, near_hop = tied([v[: second - third] for v in near_hop], near_hop)
        near_second = onward(farther)
        low_near = low_of(1, third, near_hop, down)
        (low_near,), third_hop = tied([low_near], third_hop)
        farthest, third_hop = tied([v[:far] for v in third_hop], third_hop)
        fourth_hop = onward(farthest)
        low_3 = low_of(3, 0, third_hop, down)
        (low_3,), near_second = tied([low_3], near_second)
        back_3 = onward(both_ways(low_3, 3, 0), -3)
        low_near_2 = low_of(2, third, near_second, down)
        (low_near_2,), fourth_hop = tied([low_near_2], fourth_hop)
        delta_near_2 = both_ways(low_near_2, 2, third)
        back_2 = onward(
            [jnp.concatenate(v, 0) for v in zip(both_ways(low_2, 2, 0), delta_near_2)], -1
        )
        delta_4 = both_ways(low_of(4, 0, fourth_hop, down), 4, 0)
        back_4 = onward(delta_4, -4)
        _, back_2, back_3 = tied(delta_4, back_2, back_3)
        back = [jnp.concatenate(v, 0) for v in zip(both_ways(low_1, 1, 0), both_ways(low_near, 1, third))]
        back = onward(added(back_2, back), -1)
        back = added(back_4, added(back_3, back))
        own_delta = delta_of(own_low, own_label)
        finished = jnp.concatenate([*back, own_delta], 0)
        column = jnp.where(
            slot < chip_rows,
            slot,
            jnp.where(
                slot < 2 * chip_rows,
                slot - chip_rows + most_rows,
                slot - 2 * chip_rows + 2 * most_rows,
            ),
        )
        hit = (column[:, None] == jnp.arange(finished.shape[0], dtype=jnp.int32)[None, :]).astype(
            jnp.bfloat16
        )

        def taken(h):
            return jnp.dot(h, finished, preferred_element_type=jnp.float32).astype(jnp.bfloat16)

        given = across(taken(hit[rows:]))
        kept = taken(hit[:rows])
        delta = jnp.where(
            core == 0,
            jnp.concatenate([kept, given], 1),
            jnp.concatenate([given, kept], 1),
        )
        return (base + delta.astype(jnp.float32)).astype(jnp.bfloat16)

    given = (
        lax.optimization_barrier(features),
        slot,
        slots_here,
        items_here,
        tokens,
        base_value_weight,
        down_factors,
        down_other,
        up_factors,
        up_other,
        jnp.concatenate([adapter_scales, other_scales], 0),
    )
    values = exchange(usual, *given)
    return lax.cond(
        overfull,
        lambda kept, *rest: exchange(largest, *rest),
        lambda kept, *rest: kept,
        values,
        *given,
    )


def by_all_to_all(
    tokens, row_adapter_index, base_value_weight, down_factors, up_factors, adapter_scales
):
    peers = lax.axis_size("replica")
    input_rows = tokens.shape[0]
    feature_width = tokens.shape[1]
    rows_per_replica = down_factors.shape[0]
    rank_index = down_factors.shape[1]
    capacity = 3 * input_rows // peers
    slots = peers * capacity
    holder = row_adapter_index // rows_per_replica
    local_slot = row_adapter_index % rows_per_replica
    dest_table = (holder[:, None] == jnp.arange(peers, dtype=jnp.int32)[None, :]).astype(jnp.int32)
    position = jnp.sum(jnp.cumsum(dest_table, axis=0) * dest_table, axis=1) - 1
    target = holder * capacity + position
    outbox = jnp.zeros((slots, feature_width), tokens.dtype).at[target].set(tokens)
    labels = jnp.full((slots,), -1, jnp.int32).at[target].set(local_slot)
    inbox, in_labels = (
        lax.all_to_all(
            outbox.reshape(peers, capacity, feature_width),
            "replica",
            split_axis=0,
            concat_axis=0,
            tiled=True,
        ),
        lax.all_to_all(
            labels.reshape(peers, capacity), "replica", split_axis=0, concat_axis=0, tiled=True
        ),
    )
    received = inbox.reshape(slots, feature_width)
    marks = in_labels.reshape(slots)
    selected_adapters = (
        marks[:, None] == jnp.arange(rows_per_replica, dtype=jnp.int32)[None, :]
    ).astype(jnp.float32)
    stacked_down_factors = down_factors.reshape(rows_per_replica * rank_index, feature_width)
    wide = lax.dot_general(
        received, stacked_down_factors, (((1,), (1,)), ((), ())), preferred_element_type=jnp.float32
    )
    partial_low = jnp.sum(
        wide.reshape(slots, rows_per_replica, rank_index) * selected_adapters[:, :, None], axis=1
    )
    low_rank_output = lax.psum(partial_low, "tensor")
    scale_factor = jnp.sum(selected_adapters * adapter_scales[None, :], axis=1)
    scaled_output = (low_rank_output * scale_factor[:, None]).astype(jnp.bfloat16)
    spread_rows = (
        scaled_output[:, None, :] * selected_adapters[:, :, None].astype(jnp.bfloat16)
    ).reshape(slots, rows_per_replica * rank_index)
    delta = jnp.dot(
        spread_rows,
        up_factors.reshape(rows_per_replica * rank_index, up_factors.shape[2]),
        preferred_element_type=jnp.float32,
    )
    base_part = jnp.dot(received, base_value_weight, preferred_element_type=jnp.float32)
    base_cols = lax.psum_scatter(base_part, "tensor", scatter_dimension=1, tiled=True)
    finished = base_cols + delta
    returned = lax.all_to_all(
        finished.reshape(peers, capacity, finished.shape[1]).astype(jnp.bfloat16),
        "replica",
        split_axis=0,
        concat_axis=0,
        tiled=True,
    ).astype(jnp.float32)
    total = returned.reshape(slots, finished.shape[1])[target]
    return total.astype(jnp.bfloat16)


def solution(mesh):
    in_specs = (
        P(("groups", "replica"), "tensor"),
        P(("groups", "replica")),
        P("tensor", None),
        P("replica", None, "tensor"),
        P("replica", None, "tensor"),
        P("replica"),
    )
    out_specs = P(("groups", "replica"), "tensor")
    whole_rows = mesh.shape["tensor"] == 1 and mesh.shape["replica"] == 16
    return jax.shard_map(
        by_ring if whole_rows else by_all_to_all,
        mesh=mesh,
        in_specs=in_specs,
        out_specs=out_specs,
        check_vma=False,
    )
```

```python
import jax
import jax.numpy as jnp
from jax import lax
from jax.sharding import PartitionSpec as P


def sizes_for(rows, cap):
    chip_rows = 2 * rows
    unit = chip_rows // 32
    usual = tuple(unit * s for s in (23, 18, 12, 6))
    return usual, (chip_rows, chip_rows, min(chip_rows, 2 * cap), cap)


def tied(*groups):
    flat = [v for g in groups for v in g]
    flat = list(lax.optimization_barrier(tuple(flat)))
    out = []
    for g in groups:
        out.append(flat[: len(g)])
        flat = flat[len(g) :]
    return out


def by_ring(tokens, row_adapter_index, base_value_weight, down_factors, up_factors, adapter_scales):
    rows, width = tokens.shape
    own_adapters, rank, _ = down_factors.shape
    cols = base_value_weight.shape[1]
    half, half_cols = width // 2, cols // 2
    peers = lax.axis_size("replica")
    chips = peers // 2
    lines = chips // 2
    hops = chips // 2
    adapters = 2 * own_adapters
    chip_rows = 2 * rows
    cap = 4 * (3 * rows // peers)
    usual, largest = sizes_for(rows, cap)
    me = lax.axis_index("replica")
    core = me % 2
    order = [2 * z for z in range(lines)] + [2 * z + 1 for z in reversed(range(lines))]

    def place(c):
        return jnp.where(c % 2 == 0, c // 2, chips - 1 - c // 2)

    here = place(me // 2)

    def across(v):
        return lax.ppermute(v, "replica", [(i, i ^ 1) for i in range(peers)])

    def around(v, step):
        moves = [
            (2 * order[p] + c, 2 * order[(p + step) % chips] + c)
            for p in range(chips)
            for c in range(2)
        ]
        return lax.ppermute(v, "replica", moves)

    groups = lax.axis_size("groups")
    with jax.named_scope("other_core"):
        other_tokens = across(tokens)
        other_scales = across(adapter_scales)
        up_other = across(up_factors)
        (down_late,), (other_tokens, other_scales, up_other) = tied(
            [down_factors], [other_tokens, other_scales, up_other]
        )
        down_other = across(down_late)

    with jax.named_scope("indices"):
        outgoing = jnp.broadcast_to(row_adapter_index[None, :], (groups * peers, rows))
        every = lax.all_to_all(
            outgoing, ("groups", "replica"), split_axis=0, concat_axis=0, tiled=True
        ).reshape(groups * chips, chip_rows)

    def half_of(v, axis):
        size = v.shape[axis] // 2
        return lax.dynamic_slice_in_dim(v, core * size, size, axis)

    features = jnp.concatenate([half_of(tokens, 1), half_of(other_tokens, 1)], 0)

    kind = jnp.arange(chips)[None, :]
    spot = jnp.arange(chip_rows, dtype=jnp.int32)
    earlier = (spot[None, :] < spot[:, None]).astype(jnp.bfloat16)

    def slots_of(index, position):
        distance = (place(index // adapters) - position) % chips
        marks = distance[:, :, None] == jnp.arange(chips)[None, None, :]
        ahead = jnp.einsum(
            "rs,gsk->grk", earlier, marks.astype(jnp.bfloat16), preferred_element_type=jnp.float32
        )
        marks_f = marks.astype(jnp.float32)
        rank_in = jnp.sum(ahead * marks_f, axis=2)
        count = jnp.sum(marks_f, axis=1)

        def over(mask):
            return jnp.sum(count * mask, axis=1, keepdims=True)

        right = [over((kind >= h) & (kind < hops)) for h in range(1, hops)]
        left = [over((kind > hops) & (kind <= chips - h)) for h in range(1, hops)]
        at_far = count[:, hops : hops + 1]
        right_room = jnp.full_like(at_far, usual[-1])
        left_room = right_room
        for h in range(1, hops):
            right_room = jnp.minimum(right_room, usual[h - 1] - right[h - 1])
            left_room = jnp.minimum(left_room, usual[h - 1] - left[h - 1])
        split = jnp.floor((sum(left) - sum(right) + hops * at_far) / (2.0 * hops))
        split = jnp.minimum(jnp.maximum(split, at_far - left_room), right_room)
        split = jnp.clip(split, 0.0, at_far)
        most = [jnp.maximum(r + split, l + at_far - split) for r, l in zip(right, left)]
        most = jnp.concatenate(most + [jnp.maximum(split, at_far - split)], 1)
        slot = rank_in + jnp.where(
            distance == 0,
            2.0 * chip_rows,
            jnp.where((distance == hops) & (rank_in >= split), chip_rows - split, 0.0),
        )
        for h in range(1, hops):
            beyond = right[h] if h + 1 < hops else 0.0
            slot = slot + jnp.where(distance == h, beyond + split, 0.0)
            beyond = left[h] if h + 1 < hops else 0.0
            slot = slot + jnp.where(distance == chips - h, beyond + at_far - split + chip_rows, 0.0)
        return slot.astype(jnp.int32), distance, most

    with jax.named_scope("all_slots"):
        positions = place(jnp.arange(groups * chips, dtype=jnp.int32) % chips)[:, None]
        all_slots, all_distances, most = slots_of(every, positions)
        overfull = jnp.any(most > jnp.asarray([usual], jnp.float32))

        def from_here(table):
            table = lax.dynamic_slice_in_dim(table, lax.axis_index("groups") * chips, chips, 0)
            ring = [table[c : c + 1] for c in order]
            return lax.dynamic_slice_in_dim(jnp.concatenate(ring + ring, 0), here, chips, 0)

        slots_here = from_here(all_slots)
        slot = jnp.where(core == 0, slots_here[0], jnp.roll(slots_here[0], rows))
        toward = (chips - jnp.arange(chips, dtype=jnp.int32))[:, None] % chips
        items_here = jnp.where(
            from_here(all_distances) == toward, from_here(every % adapters) + 1, 0
        )

    ways = (1, -1)

    def labels(tables, side, line, first, size):
        slots_here, items_here = tables
        at = side + first + jnp.arange(size, dtype=jnp.int32)
        hit = at[:, None] == slots_here[line][None, :]
        return jnp.sum(jnp.where(hit, items_here[line][None, :], 0), axis=1) - 1

    def chosen_by(label):
        turned = jnp.where(core == 0, label, (label + own_adapters) % adapters)
        return (label >= 0)[:, None] & (turned[:, None] == jnp.arange(adapters)[None, :])

    def packed(features, slot, base, first, size):
        hit = (base + first + jnp.arange(size, dtype=jnp.int32))[:, None] == slot[None, :]
        return jnp.dot(
            hit.astype(jnp.bfloat16), features, preferred_element_type=jnp.float32
        ).astype(jnp.bfloat16)

    def low_part(x, label, down):
        chosen = chosen_by(label)
        wide = lax.dot_general(
            x, down, (((1,), (1,)), ((), ())), preferred_element_type=jnp.float32
        )
        return jnp.sum(
            wide.reshape(x.shape[0], adapters, rank) * chosen.astype(jnp.float32)[:, :, None],
            axis=1,
        )

    def exchange(tier, features, slot, slots_here, items_here, tokens, weight, down_own, down_other, up_own, up_other, scales):
        most_rows, second, third, far = tier

        def part(slot, first, last):
            return [
                packed(features, slot, 0 if d > 0 else chip_rows, first, last - first)
                for d in ways
            ]

        def onward(blocks, step=1):
            return [around(v, step * d) for v, d in zip(blocks, ways)]

        def label_of(h, first, size):
            return jnp.concatenate(
                [
                    labels(tables, 0, chips - h, first, size),
                    labels(tables, chip_rows, h, first, size),
                ],
                0,
            )

        def low_of(h, first, blocks, down):
            label = label_of(h, first, blocks[0].shape[0])
            return low_part(jnp.concatenate(blocks, 0), label, down)

        def delta_of(low, label):
            chosen = chosen_by(label)
            total = low + across(low)
            factor = jnp.sum(jnp.where(chosen, scales[None, :], 0.0), axis=1)
            scaled = (total * factor[:, None]).astype(jnp.bfloat16)
            spread = (scaled[:, None, :] * chosen.astype(jnp.bfloat16)[:, :, None]).reshape(
                -1, adapters * rank
            )
            return jnp.dot(spread, up, preferred_element_type=jnp.float32).astype(jnp.bfloat16)

        def both_ways(low, h, first):
            size = low.shape[0] // 2
            delta = delta_of(low, label_of(h, first, size))
            return [delta[:size], delta[size:]]

        def added(small, large):
            return [
                b + jnp.pad(a, ((0, b.shape[0] - a.shape[0]), (0, 0)))
                for a, b in zip(small, large)
            ]

        sent = part(slot, 0, third)
        (down_own, up_own, slot_late), sent = tied([down_own, up_own, slot], sent)
        first_hop = onward(sent)
        down = jnp.concatenate([half_of(down_own, 2), half_of(down_other, 2)], 0)
        down = down.reshape(adapters * rank, half)
        up = jnp.concatenate([half_of(up_own, 2), half_of(up_other, 2)], 0)
        up = up.reshape(adapters * rank, half_cols)
        near = part(slot_late, third, most_rows)
        own_rows = packed(features, slot_late, 2 * chip_rows, 0, cap)
        tables, (own_rows,) = tied([slots_here, items_here], [own_rows])
        own_label = labels(tables, 2 * chip_rows, 0, 0, cap)
        (tokens, down, up, own_rows, *near), first_hop = tied(
            [tokens, down, up, own_rows, *near], first_hop
        )
        second_hop = onward(first_hop)
        near_hop = onward(near)
        low_1 = low_of(1, 0, first_hop, down)
        own_low = low_part(own_rows, own_label, down)
        base = jnp.dot(tokens, weight, preferred_element_type=jnp.float32)
        (low_1, own_low, base), second_hop = tied([low_1, own_low, base], second_hop)
        third_hop = onward(second_hop)
        low_2 = low_of(2, 0, second_hop, down)
        (low_2,), near_hop = tied([low_2], near_hop)
        farther, near_hop = tied([v[: second - third] for v in near_hop], near_hop)
        near_second = onward(farther)
        low_near = low_of(1, third, near_hop, down)
        (low_near,), third_hop = tied([low_near], third_hop)
        farthest, third_hop = tied([v[:far] for v in third_hop], third_hop)
        fourth_hop = onward(farthest)
        low_3 = low_of(3, 0, third_hop, down)
        (low_3,), near_second = tied([low_3], near_second)
        back_3 = onward(both_ways(low_3, 3, 0), -3)
        low_near_2 = low_of(2, third, near_second, down)
        delta_near_2 = both_ways(low_near_2, 2, third)
        delta_near_2, fourth_hop = tied(delta_near_2, fourth_hop)
        back_2 = onward(
            [jnp.concatenate(v, 0) for v in zip(both_ways(low_2, 2, 0), delta_near_2)], -1
        )
        delta_4 = both_ways(low_of(4, 0, fourth_hop, down), 4, 0)
        back_4 = onward(delta_4, -4)
        _, back_2, back_3 = tied(delta_4, back_2, back_3)
        back = [jnp.concatenate(v, 0) for v in zip(both_ways(low_1, 1, 0), both_ways(low_near, 1, third))]
        back = onward(added(back_2, back), -1)
        back = added(back_4, added(back_3, back))
        own_delta = delta_of(own_low, own_label)
        finished = jnp.concatenate([*back, own_delta], 0)
        column = jnp.where(
            slot < chip_rows,
            slot,
            jnp.where(
                slot < 2 * chip_rows,
                slot - chip_rows + most_rows,
                slot - 2 * chip_rows + 2 * most_rows,
            ),
        )
        hit = (column[:, None] == jnp.arange(finished.shape[0], dtype=jnp.int32)[None, :]).astype(
            jnp.bfloat16
        )

        def taken(h):
            return jnp.dot(h, finished, preferred_element_type=jnp.float32).astype(jnp.bfloat16)

        given = across(taken(hit[rows:]))
        kept = taken(hit[:rows])
        delta = jnp.where(
            core == 0,
            jnp.concatenate([kept, given], 1),
            jnp.concatenate([given, kept], 1),
        )
        return (base + delta.astype(jnp.float32)).astype(jnp.bfloat16)

    given = (
        lax.optimization_barrier(features),
        slot,
        slots_here,
        items_here,
        tokens,
        base_value_weight,
        down_factors,
        down_other,
        up_factors,
        up_other,
        jnp.concatenate([adapter_scales, other_scales], 0),
    )
    values = exchange(usual, *given)
    return lax.cond(
        overfull,
        lambda kept, *rest: exchange(largest, *rest),
        lambda kept, *rest: kept,
        values,
        *given,
    )


def by_all_to_all(
    tokens, row_adapter_index, base_value_weight, down_factors, up_factors, adapter_scales
):
    peers = lax.axis_size("replica")
    input_rows = tokens.shape[0]
    feature_width = tokens.shape[1]
    rows_per_replica = down_factors.shape[0]
    rank_index = down_factors.shape[1]
    capacity = 3 * input_rows // peers
    slots = peers * capacity
    holder = row_adapter_index // rows_per_replica
    local_slot = row_adapter_index % rows_per_replica
    dest_table = (holder[:, None] == jnp.arange(peers, dtype=jnp.int32)[None, :]).astype(jnp.int32)
    position = jnp.sum(jnp.cumsum(dest_table, axis=0) * dest_table, axis=1) - 1
    target = holder * capacity + position
    outbox = jnp.zeros((slots, feature_width), tokens.dtype).at[target].set(tokens)
    labels = jnp.full((slots,), -1, jnp.int32).at[target].set(local_slot)
    inbox, in_labels = (
        lax.all_to_all(
            outbox.reshape(peers, capacity, feature_width),
            "replica",
            split_axis=0,
            concat_axis=0,
            tiled=True,
        ),
        lax.all_to_all(
            labels.reshape(peers, capacity), "replica", split_axis=0, concat_axis=0, tiled=True
        ),
    )
    received = inbox.reshape(slots, feature_width)
    marks = in_labels.reshape(slots)
    selected_adapters = (
        marks[:, None] == jnp.arange(rows_per_replica, dtype=jnp.int32)[None, :]
    ).astype(jnp.float32)
    stacked_down_factors = down_factors.reshape(rows_per_replica * rank_index, feature_width)
    wide = lax.dot_general(
        received, stacked_down_factors, (((1,), (1,)), ((), ())), preferred_element_type=jnp.float32
    )
    partial_low = jnp.sum(
        wide.reshape(slots, rows_per_replica, rank_index) * selected_adapters[:, :, None], axis=1
    )
    low_rank_output = lax.psum(partial_low, "tensor")
    scale_factor = jnp.sum(selected_adapters * adapter_scales[None, :], axis=1)
    scaled_output = (low_rank_output * scale_factor[:, None]).astype(jnp.bfloat16)
    spread_rows = (
        scaled_output[:, None, :] * selected_adapters[:, :, None].astype(jnp.bfloat16)
    ).reshape(slots, rows_per_replica * rank_index)
    delta = jnp.dot(
        spread_rows,
        up_factors.reshape(rows_per_replica * rank_index, up_factors.shape[2]),
        preferred_element_type=jnp.float32,
    )
    base_part = jnp.dot(received, base_value_weight, preferred_element_type=jnp.float32)
    base_cols = lax.psum_scatter(base_part, "tensor", scatter_dimension=1, tiled=True)
    finished = base_cols + delta
    returned = lax.all_to_all(
        finished.reshape(peers, capacity, finished.shape[1]).astype(jnp.bfloat16),
        "replica",
        split_axis=0,
        concat_axis=0,
        tiled=True,
    ).astype(jnp.float32)
    total = returned.reshape(slots, finished.shape[1])[target]
    return total.astype(jnp.bfloat16)


def solution(mesh):
    in_specs = (
        P(("groups", "replica"), "tensor"),
        P(("groups", "replica")),
        P("tensor", None),
        P("replica", None, "tensor"),
        P("replica", None, "tensor"),
        P("replica"),
    )
    out_specs = P(("groups", "replica"), "tensor")
    whole_rows = mesh.shape["tensor"] == 1 and mesh.shape["replica"] == 16
    return jax.shard_map(
        by_ring if whole_rows else by_all_to_all,
        mesh=mesh,
        in_specs=in_specs,
        out_specs=out_specs,
        check_vma=False,
    )
```

```python
import jax
import jax.numpy as jnp
from jax import lax
from jax.sharding import PartitionSpec as P


def sizes_for(rows, cap):
    chip_rows = 2 * rows
    unit = chip_rows // 32
    usual = tuple(unit * s for s in (23, 18, 12, 6))
    return usual, (chip_rows, chip_rows, min(chip_rows, 2 * cap), cap)


def tied(*groups):
    flat = [v for g in groups for v in g]
    flat = list(lax.optimization_barrier(tuple(flat)))
    out = []
    for g in groups:
        out.append(flat[: len(g)])
        flat = flat[len(g) :]
    return out


def by_ring(tokens, row_adapter_index, base_value_weight, down_factors, up_factors, adapter_scales):
    rows, width = tokens.shape
    own_adapters, rank, _ = down_factors.shape
    cols = base_value_weight.shape[1]
    half, half_cols = width // 2, cols // 2
    peers = lax.axis_size("replica")
    chips = peers // 2
    lines = chips // 2
    hops = chips // 2
    adapters = 2 * own_adapters
    chip_rows = 2 * rows
    cap = 4 * (3 * rows // peers)
    usual, largest = sizes_for(rows, cap)
    me = lax.axis_index("replica")
    core = me % 2
    order = [2 * z for z in range(lines)] + [2 * z + 1 for z in reversed(range(lines))]

    def place(c):
        return jnp.where(c % 2 == 0, c // 2, chips - 1 - c // 2)

    here = place(me // 2)

    def across(v):
        return lax.ppermute(v, "replica", [(i, i ^ 1) for i in range(peers)])

    def around(v, step):
        moves = [
            (2 * order[p] + c, 2 * order[(p + step) % chips] + c)
            for p in range(chips)
            for c in range(2)
        ]
        return lax.ppermute(v, "replica", moves)

    groups = lax.axis_size("groups")
    with jax.named_scope("other_core"):
        other_tokens = across(tokens)
        other_scales = across(adapter_scales)
        up_other = across(up_factors)
        (down_late,), (other_tokens, other_scales, up_other) = tied(
            [down_factors], [other_tokens, other_scales, up_other]
        )
        down_other = across(down_late)

    with jax.named_scope("indices"):
        outgoing = jnp.broadcast_to(row_adapter_index[None, :], (groups * peers, rows))
        every = lax.all_to_all(
            outgoing, ("groups", "replica"), split_axis=0, concat_axis=0, tiled=True
        ).reshape(groups * chips, chip_rows)

    def half_of(v, axis):
        size = v.shape[axis] // 2
        return lax.dynamic_slice_in_dim(v, core * size, size, axis)

    features = jnp.concatenate([half_of(tokens, 1), half_of(other_tokens, 1)], 0)

    kind = jnp.arange(chips)[None, :]
    spot = jnp.arange(chip_rows, dtype=jnp.int32)
    earlier = (spot[None, :] < spot[:, None]).astype(jnp.bfloat16)

    def slots_of(index, position):
        distance = (place(index // adapters) - position) % chips
        marks = distance[:, :, None] == jnp.arange(chips)[None, None, :]
        ahead = jnp.einsum(
            "rs,gsk->grk", earlier, marks.astype(jnp.bfloat16), preferred_element_type=jnp.float32
        )
        marks_f = marks.astype(jnp.float32)
        rank_in = jnp.sum(ahead * marks_f, axis=2)
        count = jnp.sum(marks_f, axis=1)

        def over(mask):
            return jnp.sum(count * mask, axis=1, keepdims=True)

        right = [over((kind >= h) & (kind < hops)) for h in range(1, hops)]
        left = [over((kind > hops) & (kind <= chips - h)) for h in range(1, hops)]
        at_far = count[:, hops : hops + 1]
        right_room = jnp.full_like(at_far, usual[-1])
        left_room = right_room
        for h in range(1, hops):
            right_room = jnp.minimum(right_room, usual[h - 1] - right[h - 1])
            left_room = jnp.minimum(left_room, usual[h - 1] - left[h - 1])
        split = jnp.floor((sum(left) - sum(right) + hops * at_far) / (2.0 * hops))
        split = jnp.minimum(jnp.maximum(split, at_far - left_room), right_room)
        split = jnp.clip(split, 0.0, at_far)
        most = [jnp.maximum(r + split, l + at_far - split) for r, l in zip(right, left)]
        most = jnp.concatenate(most + [jnp.maximum(split, at_far - split)], 1)
        slot = rank_in + jnp.where(
            distance == 0,
            2.0 * chip_rows,
            jnp.where((distance == hops) & (rank_in >= split), chip_rows - split, 0.0),
        )
        for h in range(1, hops):
            beyond = right[h] if h + 1 < hops else 0.0
            slot = slot + jnp.where(distance == h, beyond + split, 0.0)
            beyond = left[h] if h + 1 < hops else 0.0
            slot = slot + jnp.where(distance == chips - h, beyond + at_far - split + chip_rows, 0.0)
        return slot.astype(jnp.int32), distance, most

    with jax.named_scope("all_slots"):
        positions = place(jnp.arange(groups * chips, dtype=jnp.int32) % chips)[:, None]
        all_slots, all_distances, most = slots_of(every, positions)
        overfull = jnp.any(most > jnp.asarray([usual], jnp.float32))

        def from_here(table):
            table = lax.dynamic_slice_in_dim(table, lax.axis_index("groups") * chips, chips, 0)
            ring = [table[c : c + 1] for c in order]
            return lax.dynamic_slice_in_dim(jnp.concatenate(ring + ring, 0), here, chips, 0)

        slots_here = from_here(all_slots)
        slot = jnp.where(core == 0, slots_here[0], jnp.roll(slots_here[0], rows))
        toward = (chips - jnp.arange(chips, dtype=jnp.int32))[:, None] % chips
        items_here = jnp.where(
            from_here(all_distances) == toward, from_here(every % adapters) + 1, 0
        )

    ways = (1, -1)

    def labels(tables, side, line, first, size):
        slots_here, items_here = tables
        at = side + first + jnp.arange(size, dtype=jnp.int32)
        hit = at[:, None] == slots_here[line][None, :]
        return jnp.sum(jnp.where(hit, items_here[line][None, :], 0), axis=1) - 1

    def chosen_by(label):
        turned = jnp.where(core == 0, label, (label + own_adapters) % adapters)
        return (label >= 0)[:, None] & (turned[:, None] == jnp.arange(adapters)[None, :])

    def packed(features, slot, base, first, size):
        hit = (base + first + jnp.arange(size, dtype=jnp.int32))[:, None] == slot[None, :]
        return jnp.dot(
            hit.astype(jnp.bfloat16), features, preferred_element_type=jnp.float32
        ).astype(jnp.bfloat16)

    def low_part(x, label, down):
        chosen = chosen_by(label)
        wide = lax.dot_general(
            x, down, (((1,), (1,)), ((), ())), preferred_element_type=jnp.float32
        )
        return jnp.sum(
            wide.reshape(x.shape[0], adapters, rank) * chosen.astype(jnp.float32)[:, :, None],
            axis=1,
        )

    def exchange(tier, features, slot, slots_here, items_here, tokens, weight, down_own, down_other, up_own, up_other, scales):
        most_rows, second, third, far = tier

        def part(slot, first, last):
            return [
                packed(features, slot, 0 if d > 0 else chip_rows, first, last - first)
                for d in ways
            ]

        def onward(blocks, step=1):
            return [around(v, step * d) for v, d in zip(blocks, ways)]

        def label_of(h, first, size):
            return jnp.concatenate(
                [
                    labels(tables, 0, chips - h, first, size),
                    labels(tables, chip_rows, h, first, size),
                ],
                0,
            )

        def low_of(h, first, blocks, down):
            label = label_of(h, first, blocks[0].shape[0])
            return low_part(jnp.concatenate(blocks, 0), label, down)

        def delta_of(low, label):
            chosen = chosen_by(label)
            total = low + across(low)
            factor = jnp.sum(jnp.where(chosen, scales[None, :], 0.0), axis=1)
            scaled = (total * factor[:, None]).astype(jnp.bfloat16)
            spread = (scaled[:, None, :] * chosen.astype(jnp.bfloat16)[:, :, None]).reshape(
                -1, adapters * rank
            )
            return jnp.dot(spread, up, preferred_element_type=jnp.float32).astype(jnp.bfloat16)

        def both_ways(low, h, first):
            size = low.shape[0] // 2
            delta = delta_of(low, label_of(h, first, size))
            return [delta[:size], delta[size:]]

        def added(small, large):
            return [
                b + jnp.pad(a, ((0, b.shape[0] - a.shape[0]), (0, 0)))
                for a, b in zip(small, large)
            ]

        sent = part(slot, 0, third)
        (down_own, up_own, slot_late), sent = tied([down_own, up_own, slot], sent)
        first_hop = onward(sent)
        down = jnp.concatenate([half_of(down_own, 2), half_of(down_other, 2)], 0)
        down = down.reshape(adapters * rank, half)
        up = jnp.concatenate([half_of(up_own, 2), half_of(up_other, 2)], 0)
        up = up.reshape(adapters * rank, half_cols)
        near = part(slot_late, third, most_rows)
        own_rows = packed(features, slot_late, 2 * chip_rows, 0, cap)
        tables, (own_rows,) = tied([slots_here, items_here], [own_rows])
        own_label = labels(tables, 2 * chip_rows, 0, 0, cap)
        (tokens, down, up, own_rows, *near), first_hop = tied(
            [tokens, down, up, own_rows, *near], first_hop
        )
        second_hop = onward(first_hop)
        near_hop = onward(near)
        low_1 = low_of(1, 0, first_hop, down)
        own_low = low_part(own_rows, own_label, down)
        base = jnp.dot(tokens, weight, preferred_element_type=jnp.float32)
        (low_1, own_low, base), second_hop = tied([low_1, own_low, base], second_hop)
        third_hop = onward(second_hop)
        low_2 = low_of(2, 0, second_hop, down)
        (low_2,), near_hop = tied([low_2], near_hop)
        farther, near_hop = tied([v[: second - third] for v in near_hop], near_hop)
        near_second = onward(farther)
        low_near = low_of(1, third, near_hop, down)
        (low_near,), third_hop = tied([low_near], third_hop)
        farthest, third_hop = tied([v[:far] for v in third_hop], third_hop)
        fourth_hop = onward(farthest)
        low_3 = low_of(3, 0, third_hop, down)
        (low_3,), near_second = tied([low_3], near_second)
        back_3 = onward(both_ways(low_3, 3, 0), -3)
        low_near_2 = low_of(2, third, near_second, down)
        (low_near_2,), fourth_hop = tied([low_near_2], fourth_hop)
        delta_near_2 = both_ways(low_near_2, 2, third)
        back_2 = onward(
            [jnp.concatenate(v, 0) for v in zip(both_ways(low_2, 2, 0), delta_near_2)], -1
        )
        delta_4 = both_ways(low_of(4, 0, fourth_hop, down), 4, 0)
        delta_4, back_3 = tied(delta_4, back_3)
        back_4 = onward(delta_4, -4)
        back_4, back_2 = tied(back_4, back_2)
        back = [jnp.concatenate(v, 0) for v in zip(both_ways(low_1, 1, 0), both_ways(low_near, 1, third))]
        back = onward(added(back_2, back), -1)
        back = added(back_4, added(back_3, back))
        own_delta = delta_of(own_low, own_label)
        finished = jnp.concatenate([*back, own_delta], 0)
        column = jnp.where(
            slot < chip_rows,
            slot,
            jnp.where(
                slot < 2 * chip_rows,
                slot - chip_rows + most_rows,
                slot - 2 * chip_rows + 2 * most_rows,
            ),
        )
        hit = (column[:, None] == jnp.arange(finished.shape[0], dtype=jnp.int32)[None, :]).astype(
            jnp.bfloat16
        )

        def taken(h):
            return jnp.dot(h, finished, preferred_element_type=jnp.float32).astype(jnp.bfloat16)

        given = across(taken(hit[rows:]))
        kept = taken(hit[:rows])
        delta = jnp.where(
            core == 0,
            jnp.concatenate([kept, given], 1),
            jnp.concatenate([given, kept], 1),
        )
        return (base + delta.astype(jnp.float32)).astype(jnp.bfloat16)

    given = (
        lax.optimization_barrier(features),
        slot,
        slots_here,
        items_here,
        tokens,
        base_value_weight,
        down_factors,
        down_other,
        up_factors,
        up_other,
        jnp.concatenate([adapter_scales, other_scales], 0),
    )
    values = exchange(usual, *given)
    return lax.cond(
        overfull,
        lambda kept, *rest: exchange(largest, *rest),
        lambda kept, *rest: kept,
        values,
        *given,
    )


def by_all_to_all(
    tokens, row_adapter_index, base_value_weight, down_factors, up_factors, adapter_scales
):
    peers = lax.axis_size("replica")
    input_rows = tokens.shape[0]
    feature_width = tokens.shape[1]
    rows_per_replica = down_factors.shape[0]
    rank_index = down_factors.shape[1]
    capacity = 3 * input_rows // peers
    slots = peers * capacity
    holder = row_adapter_index // rows_per_replica
    local_slot = row_adapter_index % rows_per_replica
    dest_table = (holder[:, None] == jnp.arange(peers, dtype=jnp.int32)[None, :]).astype(jnp.int32)
    position = jnp.sum(jnp.cumsum(dest_table, axis=0) * dest_table, axis=1) - 1
    target = holder * capacity + position
    outbox = jnp.zeros((slots, feature_width), tokens.dtype).at[target].set(tokens)
    labels = jnp.full((slots,), -1, jnp.int32).at[target].set(local_slot)
    inbox, in_labels = (
        lax.all_to_all(
            outbox.reshape(peers, capacity, feature_width),
            "replica",
            split_axis=0,
            concat_axis=0,
            tiled=True,
        ),
        lax.all_to_all(
            labels.reshape(peers, capacity), "replica", split_axis=0, concat_axis=0, tiled=True
        ),
    )
    received = inbox.reshape(slots, feature_width)
    marks = in_labels.reshape(slots)
    selected_adapters = (
        marks[:, None] == jnp.arange(rows_per_replica, dtype=jnp.int32)[None, :]
    ).astype(jnp.float32)
    stacked_down_factors = down_factors.reshape(rows_per_replica * rank_index, feature_width)
    wide = lax.dot_general(
        received, stacked_down_factors, (((1,), (1,)), ((), ())), preferred_element_type=jnp.float32
    )
    partial_low = jnp.sum(
        wide.reshape(slots, rows_per_replica, rank_index) * selected_adapters[:, :, None], axis=1
    )
    low_rank_output = lax.psum(partial_low, "tensor")
    scale_factor = jnp.sum(selected_adapters * adapter_scales[None, :], axis=1)
    scaled_output = (low_rank_output * scale_factor[:, None]).astype(jnp.bfloat16)
    spread_rows = (
        scaled_output[:, None, :] * selected_adapters[:, :, None].astype(jnp.bfloat16)
    ).reshape(slots, rows_per_replica * rank_index)
    delta = jnp.dot(
        spread_rows,
        up_factors.reshape(rows_per_replica * rank_index, up_factors.shape[2]),
        preferred_element_type=jnp.float32,
    )
    base_part = jnp.dot(received, base_value_weight, preferred_element_type=jnp.float32)
    base_cols = lax.psum_scatter(base_part, "tensor", scatter_dimension=1, tiled=True)
    finished = base_cols + delta
    returned = lax.all_to_all(
        finished.reshape(peers, capacity, finished.shape[1]).astype(jnp.bfloat16),
        "replica",
        split_axis=0,
        concat_axis=0,
        tiled=True,
    ).astype(jnp.float32)
    total = returned.reshape(slots, finished.shape[1])[target]
    return total.astype(jnp.bfloat16)


def solution(mesh):
    in_specs = (
        P(("groups", "replica"), "tensor"),
        P(("groups", "replica")),
        P("tensor", None),
        P("replica", None, "tensor"),
        P("replica", None, "tensor"),
        P("replica"),
    )
    out_specs = P(("groups", "replica"), "tensor")
    whole_rows = mesh.shape["tensor"] == 1 and mesh.shape["replica"] == 16
    return jax.shard_map(
        by_ring if whole_rows else by_all_to_all,
        mesh=mesh,
        in_specs=in_specs,
        out_specs=out_specs,
        check_vma=False,
    )
```
